32 devices in a mesh: dp: 2 (over y), pipe: 2 (over core), gz: 2 (over x), gy: 4 (over z).
Axes of the slice: x: 2, y: 2, z: 4, core: 2. Of those that a mesh axis runs over, the one named last changes fastest.
Arguments:
- volumes: bfloat16 [4, 32, 4, 32, 128], P('dp', None, 'gz', 'gy'), may hold values from -6 to 6
- conv_one: bfloat16 [32, 4, 3, 3, 3], replicated, may hold values from -0.625 to 0.625
- conv_two: bfloat16 [64, 32, 3, 3, 3], replicated, may hold values from -0.21875 to 0.21875
- cotangent: bfloat16 [4, 64, 2, 16, 64], P('dp', None, 'gz', 'gy'), may hold values from -24 to 24
Outputs:
- boundary_acts: bfloat16 [4, 32, 4, 32, 128], P('dp', None, 'gz', 'gy')
- boundary_grads: bfloat16 [4, 32, 4, 32, 128], P('dp', None, 'gz', 'gy')
- grad_conv_one: float32 [32, 4, 3, 3, 3], replicated
- grad_conv_two: float32 [64, 32, 3, 3, 3], replicated
The draws below stay inside these ranges and needn't reach their ends.
All inputs are finite; a program needn't handle non-finite values.
Results may differ from the reference program's by a relative error of at most 0.0085.
Values may be sent and summed in bfloat16 or wider, within the bound.
No kernel may reach another device: no remote copies, remote signals or barrier semaphores. Data moves between devices by JAX's collectives and lax.ppermute only.
A program may use at most 128 MiB of HBM per device.

```python
import math
import jax
import jax.numpy as jnp
from jax import lax

C_IN = 4
C_ONE = 32
C_TWO = 64
CX = 128
BATCH = 4
NZ = 4
NY = 32


def shard_levels(stream_key, dims, cuts, least, largest):
    level, own = 1.0, jax.random.fold_in(stream_key, 6)
    for axis_at, shards_of in cuts:
        draws = jnp.exp(jax.random.uniform(jax.random.fold_in(own, axis_at), (shards_of,), jnp.float32, least / len(cuts), largest / len(cuts)))
        level = level * jnp.repeat(draws, dims[axis_at] // shards_of).reshape([-1 if axis == axis_at else 1 for axis in range(len(dims))])
    return level


def gaussian(own_key, extent, width, most, shards=(), held_as=jnp.bfloat16):
    values = jax.random.normal(own_key, extent, jnp.float32) * width
    if len(shards) > 0:
        values = shard_levels(own_key, extent, shards, -0.22, 0.18) * values
    return jnp.clip(values, min=-most, max=most).astype(held_as)


def setup_inputs(seed: int = 0) -> dict:
    streams_of = jax.random.split(jax.random.key(seed), 5)
    volumes = gaussian(streams_of[0], (BATCH, 8 * C_IN, NZ, NY, CX), 1.0, 6.0, ((0, 2), (2, 2), (3, 4)))
    conv_one = gaussian(streams_of[1], (C_ONE, C_IN, 3, 3, 3), (C_IN * 27) ** -0.5, 0.625)
    conv_two = gaussian(streams_of[2], (C_TWO, C_ONE, 3, 3, 3), (C_ONE * 27) ** -0.5, 0.21875)
    cotangent = gaussian(streams_of[3], (BATCH, C_TWO, NZ // 2, NY // 2, CX // 2), 4.0, 24.0, ((0, 2), (2, 2), (3, 4)))
    return dict(volumes=volumes, conv_one=conv_one, conv_two=conv_two, cotangent=cotangent)


LEAK_SLOPE = 0.3
LOG_TWO = math.log(2.0)
LAYOUT = ('NCDHW', 'OIDHW', 'NCDHW')

def activate(pre_act):
    return LEAK_SLOPE * pre_act + (1.0 - LEAK_SLOPE) * (jax.nn.softplus(pre_act) - LOG_TWO)

def derivative(pre_act):
    return LEAK_SLOPE + (1.0 - LEAK_SLOPE) * jax.nn.sigmoid(pre_act)

def unfold(coarse):
    span_z, span_y, span_x = coarse.shape[1:]
    pieces = coarse.reshape(2, 2, 2, -1, span_z, span_y, span_x)
    ordered = pieces.transpose(3, 4, 0, 5, 1, 6, 2)
    return ordered.reshape(-1, 2 * span_z, 2 * span_y, 2 * span_x)

def average_blocks(grid_in):
    chan_count, span_z, span_y, span_x = grid_in.shape
    grouped = grid_in.reshape(chan_count, span_z // 2, 2, span_y // 2, 2, span_x // 2, 2)
    return lax.optimization_barrier(jnp.mean(grouped, axis=(2, 4, 6)))

def spread_blocks(grid_in):
    chan_count, span_z, span_y, span_x = grid_in.shape
    copied = jnp.broadcast_to(grid_in[:, :, None, :, None, :, None], (chan_count, span_z, 2, span_y, 2, span_x, 2))
    return copied.reshape(chan_count, 2 * span_z, 2 * span_y, 2 * span_x) / 8.0

def convolve(grid_in, kernel):
    result = lax.conv_general_dilated(grid_in[None], kernel, (1, 1, 1), ((1, 1), (1, 1), (1, 1)), dimension_numbers=LAYOUT, preferred_element_type=jnp.float32)
    return result[0]

def kernel_grad(padded, grad_out):
    out_count = grad_out.shape[0]
    in_count = padded.shape[0]
    span_z, span_y, span_x = grad_out.shape[1:]
    flat_out = grad_out.reshape(out_count, -1)
    products = []
    for off_z in range(3):
        for off_y in range(3):
            for off_x in range(3):
                shifted = padded[:, off_z:off_z + span_z, off_y:off_y + span_y, off_x:off_x + span_x].reshape(in_count, -1)
                products.append(jnp.dot(flat_out, shifted.T, preferred_element_type=jnp.float32))
    return jnp.stack(products, axis=-1).reshape(out_count, in_count, 3, 3, 3)

def reference(volumes, conv_one, conv_two, cotangent):
    flipped = jnp.flip(conv_two, axis=(2, 3, 4)).transpose(1, 0, 2, 3, 4)
    pad_three = ((0, 0), (1, 1), (1, 1), (1, 1))

    def per_volume(totals, sample):
        volume, cot_part = sample
        fine_grid = unfold(volume)
        first_pre = convolve(fine_grid, conv_one)
        pooled = average_blocks(activate(first_pre)).astype(jnp.bfloat16)
        second_pre = convolve(pooled, conv_two)
        second_grad = (derivative(second_pre) * spread_blocks(cot_part.astype(jnp.float32))).astype(jnp.bfloat16)
        back_grad = convolve(second_grad, flipped).astype(jnp.bfloat16)
        first_grad = (derivative(first_pre) * spread_blocks(back_grad.astype(jnp.float32))).astype(jnp.bfloat16)
        grad_one = totals[0] + kernel_grad(jnp.pad(fine_grid, pad_three), first_grad)
        grad_two = totals[1] + kernel_grad(jnp.pad(pooled, pad_three), second_grad)
        return ((grad_one, grad_two), (pooled, back_grad))
    start = (jnp.zeros(conv_one.shape, jnp.float32), jnp.zeros(conv_two.shape, jnp.float32))
    totals, stacked = lax.scan(per_volume, start, (volumes, cotangent))
    return (stacked[0], stacked[1], totals[0] / BATCH, totals[1] / BATCH)
```

```python
import functools

import jax
import jax.numpy as jnp
from jax import lax
from jax.experimental import pallas as pl
from jax.experimental.pallas import tpu as pltpu
from jax.sharding import PartitionSpec as P

LEAK = 0.3
REACH = 3
F32 = jnp.float32
BF16 = jnp.bfloat16
PARAMS = pltpu.CompilerParams(vmem_limit_bytes=48 * 1024 * 1024)


def pairs(count, odd):
    out = []
    for i in range(odd, count - 1, 2):
        out += [(i, i + 1), (i + 1, i)]
    return out


def swap(cells, z_count, y_count, z_pairs, y_pairs):
    z_list = [(i, i) for i in range(z_count)] if z_pairs is None else z_pairs
    y_list = [(i, i) for i in range(y_count)] if y_pairs is None else y_pairs
    perm = [(a * y_count + c, b * y_count + d) for a, b in z_list for c, d in y_list]
    return lax.ppermute(cells, ("gz", "gy"), perm)


def shift(block, step, width):
    parts = []
    for at in range(0, block.shape[1], width):
        part = block[:, at : at + width]
        lane = lax.broadcasted_iota(jnp.int32, part.shape, 1)
        edge = 0 if step > 0 else width - 1
        parts.append(jnp.where(lane == edge, 0.0, pltpu.roll(part, step % width, 1)))
    return parts[0] if len(parts) == 1 else jnp.concatenate(parts, axis=1)


class Plan:
    def __init__(self, volumes, cotangent, conv_one, conv_two):
        _, self.fold, self.z, self.y, self.x = volumes.shape
        self.c_one, self.c_in = conv_one.shape[:2]
        self.c_two = conv_two.shape[0]
        self.cz, self.cy = cotangent.shape[2:4]
        self.gz, self.gy = lax.axis_size("gz"), lax.axis_size("gy")
        self.h = min(REACH, self.z)
        sides = min(self.gz - 1, 2)
        self.win = self.z + sides * self.h
        self.planes = self.z + sides
        self.wide = self.y + 2 * REACH
        self.mid = self.y + 4
        self.slim = self.y + 2
        self.z_kinds = [None] + [k for k in (0, 1) if len(pairs(self.gz, k)) > 0]
        self.y_kinds = [None] + [k for k in (0, 1) if len(pairs(self.gy, k)) > 0]
        self.kinds = [(a, b) for a in self.z_kinds for b in self.y_kinds]

    def at_z(self):
        if self.gz > 2:
            return self.h, self.h - 1
        if self.gz == 1:
            return 0, 0
        me = lax.axis_index("gz")
        return me * self.h, me * (self.h - 1)

    def blocks(self, kind):
        z_kind, y_kind = kind
        nz, nc = (self.z, self.cz) if z_kind is None else (self.h, 1)
        ny, np_ = (self.y, self.cy // 2) if y_kind is None else (REACH, 1)
        return nz, ny, nc, np_

    def rows(self, kind):
        nz, ny, nc, np_ = self.blocks(kind)
        return nz * ny * self.fold + nc * np_ * self.c_two


def message_key(plan, kind):
    z_kind, y_kind = kind
    if z_kind is not None and plan.h == plan.z and plan.cz == 1:
        z_kind = None
    return z_kind, y_kind


def pack_kernel(plan, keys, vol_ref, cot_ref, *refs):
    out_refs, (cells, cots) = refs[: len(keys)], refs[len(keys) :]
    me = lax.axis_index("pipe")
    for z in range(plan.z):
        block = jnp.swapaxes(vol_ref[me, :, z].astype(F32), 0, 1).astype(BF16)
        for y in range(plan.y):
            cells[z, y] = block[y]
    for z in range(plan.cz):
        block = jnp.swapaxes(cot_ref[me, :, z].astype(F32), 0, 1)
        for m in range(plan.cy // 2):
            cots[z, m] = jnp.concatenate([block[2 * m], block[2 * m + 1]], axis=1).astype(BF16)
    odd_z, odd_y = lax.axis_index("gz") % 2, lax.axis_index("gy") % 2
    for key, out_ref in zip(keys, out_refs):
        nz, ny, nc, np_ = plan.blocks(key)
        z_low = 0 if key[0] is None else (odd_z == 1 - key[0])
        y_low = 0 if key[1] is None else (odd_y == 1 - key[1])
        z0 = jnp.where(z_low, 0, plan.z - nz) if key[0] is not None else 0
        c0 = jnp.where(z_low, 0, plan.cz - nc) if key[0] is not None else 0
        y0 = jnp.where(y_low, 0, plan.y - ny) if key[1] is not None else 0
        p0 = jnp.where(y_low, 0, plan.cy // 2 - np_) if key[1] is not None else 0
        at = 0
        for i in range(nz):
            for j in range(ny):
                out_ref[at : at + plan.fold] = cells[z0 + i, y0 + j]
                at += plan.fold
        for i in range(nc):
            for j in range(np_):
                out_ref[at : at + plan.c_two] = cots[c0 + i, p0 + j]
                at += plan.c_two


def weight_kernel(plan, one_ref, two_ref, w1_ref, w2_ref, wb_ref):
    c_in, c_one, c_two = plan.c_in, plan.c_one, plan.c_two
    none = jnp.zeros((c_in, c_one), F32)
    pairs_x = {}
    for dz in range(3):
        for dy in range(3):
            tap = [one_ref[(dz * 3 + dy) * 3 + dx].astype(F32) * 0.5 for dx in range(3)]
            pairs_x[dz, dy, 0] = jnp.concatenate(
                [jnp.concatenate([tap[1], tap[0]], 1), jnp.concatenate([tap[2], tap[1]], 1)], 0
            )
            pairs_x[dz, dy, 1] = jnp.concatenate(
                [jnp.concatenate([none, tap[2]], 1), jnp.concatenate([tap[0], none], 1)], 0
            )
    blank = jnp.zeros((2 * c_in, 2 * c_one), F32)
    rows = []
    for fz in range(4):
        for s in range(2):
            for fy in (1, 2, 3, 0):
                rows.append(
                    jnp.concatenate(
                        [
                            pairs_x.get((fz - a, fy - b, s), blank)
                            for a in range(2)
                            for b in range(2)
                        ],
                        axis=1,
                    )
                )
    w1_ref[...] = jnp.concatenate(rows, axis=0).T.astype(BF16)
    for dx in range(3):
        taps = [two_ref[zy * 3 + dx] for zy in range(9)]
        wb_ref[dx * c_one : (dx + 1) * c_one] = jnp.concatenate(taps, axis=1)
        tall = jnp.concatenate([t.astype(F32) * 0.5 for t in taps], axis=0)
        w2_ref[dx * c_two : (dx + 1) * c_two] = tall.T.astype(BF16)


def main_kernel(plan, count, *refs):
    msgs = refs[:count]
    w1_ref, w2_ref, wb_ref, out_ref, keep_ref, give_ref = refs[count : count + 6]
    cells, fine, act, sg, cot, tan, back, first, sgx, total = refs[count + 6 :]
    X, Y, Z = plan.x, plan.y, plan.z
    fold, c_in, c_one, c_two = plan.fold, plan.c_in, plan.c_one, plan.c_two
    me, my_z, my_y = lax.axis_index("pipe"), lax.axis_index("gz"), lax.axis_index("gy")
    own, first_sg = plan.at_z()
    odd_z, odd_y = my_z % 2, my_y % 2

    pick = (
        lax.broadcasted_iota(jnp.int32, (X, 2 * X), 1) // 2
        == lax.broadcasted_iota(jnp.int32, (X, 2 * X), 0)
    )
    pick = jnp.where(pick, 0.125, 0.0).astype(BF16)
    if plan.gz > 1:
        cot[...] = jnp.zeros_like(cot)
    for kind, msg in zip(plan.kinds, msgs):
        nz, ny, nc, np_ = plan.blocks(kind)
        z_kind, y_kind = kind
        if z_kind is None:
            z0, c0 = own, 1
        else:
            before = odd_z == 1 - z_kind
            z0 = jnp.where(before, own - plan.h, own + Z)
            z0 = jnp.clip(z0, 0, plan.win - plan.h)
            c0 = jnp.where(before, 0, plan.cz + 1)
        at = 0
        below = None if y_kind is None else odd_y == 1 - y_kind
        y0 = REACH if y_kind is None else jnp.where(below, 0, Y + REACH)
        for i in range(nz):
            for j in range(ny):
                cells[z0 + i, y0 + j] = msg[at : at + fold]
                at += fold
        for i in range(nc):
            for j in range(np_):
                up = jnp.dot(msg[at : at + c_two], pick, preferred_element_type=F32).astype(BF16)
                at += c_two
                one, two = up[:, :X], up[:, X:]
                if y_kind is None:
                    for r, piece in enumerate((one, one, two, two)):
                        lane = (4 * j + r + 1) * X
                        cot[c0 + i, :, lane : lane + X] = piece
                else:
                    lane = pl.multiple_of(jnp.where(below, 0, (Y + 1) * X), X)
                    cot[c0 + i, :, pl.ds(lane, X)] = jnp.where(below, two, one)

    quarter = 2 * c_in
    fine[0 : 8 * quarter] = jnp.zeros((8 * quarter, plan.mid * X), BF16)
    last = 8 * quarter + plan.win * 16 * quarter
    fine[last : last + 8 * quarter] = jnp.zeros((8 * quarter, plan.mid * X), BF16)
    is_c = (lax.broadcasted_iota(jnp.int32, (fold, X), 0) // c_in) % 2 == 1

    def spread(w, carry):
        base = pl.multiple_of(8 * quarter + w * 16 * quarter, 8 * quarter)
        kept = []
        for r in range(plan.wide):
            mid = cells[w, r].astype(F32)
            side = jnp.where(is_c, shift(mid, 1, X), shift(mid, -1, X))
            kept.append((mid, side))
            if r < 2:
                continue
            lane = (r - 2) * X
            for a in range(2):
                for s in range(2):
                    lo, here, hi = kept[r - 2][s], kept[r - 1][s], kept[r][s]
                    at = a * 2 * quarter
                    near = here[at : at + 2 * quarter]
                    far = jnp.concatenate(
                        [hi[at : at + quarter], lo[at + quarter : at + 2 * quarter]], axis=0
                    )
                    row = base + (a * 8 + s * 4) * quarter
                    fine[pl.ds(row, 2 * quarter), lane : lane + X] = near.astype(BF16)
                    fine[pl.ds(row + 2 * quarter, 2 * quarter), lane : lane + X] = far.astype(BF16)
        return carry

    lax.fori_loop(0, plan.win, spread, 0)

    w1 = w1_ref[...]
    act[0] = jnp.zeros(act.shape[1:], BF16)
    act[plan.win + 1] = jnp.zeros(act.shape[1:], BF16)

    def first_section(w, carry):
        row0 = pl.multiple_of(w * 16 * quarter, 8 * quarter)
        z_abs = my_z * Z + w - own
        z_ok = (z_abs >= 0) & (z_abs < plan.gz * Z)
        for q in range(plan.mid // 2):
            lane = 2 * q * X
            half = jnp.dot(
                w1, fine[pl.ds(row0, 32 * quarter), lane : lane + 2 * X], preferred_element_type=F32
            )
            line, prod = None, None
            for g in range(8):
                v = half[g * c_one : (g + 1) * c_one]
                t = jnp.tanh(v)
                if 0 < q < plan.mid // 2 - 1:
                    tan[w, g * c_one : (g + 1) * c_one, lane - 2 * X : lane] = t
                bent = jnp.maximum(v, LEAK * v)
                grown = 1.0 + jnp.abs(t)
                line = bent if line is None else line + bent
                prod = grown if prod is None else prod * grown
            mean = 0.25 * line - ((1.0 - LEAK) / 8.0) * jnp.log(prod)
            ok = z_ok
            if q == 0:
                ok = ok & (my_y > 0)
            if q == plan.mid // 2 - 1:
                ok = ok & (my_y < plan.gy - 1)
            act[w + 1, :, lane : lane + 2 * X] = jnp.where(ok, mean, 0.0).astype(BF16)
        return carry

    lax.fori_loop(0, plan.win, first_section, 0)

    w2 = w2_ref[...]
    sg[0] = jnp.zeros(sg.shape[1:], BF16)
    sg[plan.planes + 1] = jnp.zeros(sg.shape[1:], BF16)

    def around(ref, w, lane, size, sign):
        return jnp.concatenate(
            [
                ref[w + 1 + sign * dz, :, lane + sign * dy * X : lane + sign * dy * X + size]
                for dz in (-1, 0, 1)
                for dy in (-1, 0, 1)
            ],
            axis=0,
        )

    def second_section(j, carry):
        w = first_sg + j
        c_at = (w - own + 2) // 2
        for q in range(plan.slim // 2):
            lane = 2 * q * X
            taps = jnp.dot(w2, around(act, w, lane + X, 2 * X, 1), preferred_element_type=F32)
            half = (
                taps[c_two : 2 * c_two]
                + shift(taps[:c_two], 1, X)
                + shift(taps[2 * c_two :], -1, X)
            )
            slope = (LEAK + 1.0) / 2 + ((1.0 - LEAK) / 2) * jnp.tanh(half)
            part = cot[c_at, :, lane : lane + 2 * X].astype(F32)
            sg[j + 1, :, lane : lane + 2 * X] = (slope * part).astype(BF16)
        return carry

    lax.fori_loop(0, plan.planes, second_section, 0)

    grad_two = None
    for i in range(Z):
        w, j = own + i, own + i - first_sg
        for y in range(Y):
            mid = sg[j + 1, :, (y + 1) * X : (y + 2) * X]
            wide = mid.astype(F32)
            at = slice(y * X, (y + 1) * X)
            sgx[0:c_two, at] = shift(wide, -1, X).astype(BF16)
            sgx[c_two : 2 * c_two, at] = mid
            sgx[2 * c_two : 3 * c_two, at] = shift(wide, 1, X).astype(BF16)
        term = lax.dot_general(
            around(act, w, 2 * X, Y * X, 1),
            sgx[...],
            (((1,), (1,)), ((), ())),
            preferred_element_type=F32,
        )
        grad_two = term if grad_two is None else grad_two + term
    nine = 9 * c_one
    total[0:nine] = grad_two[:, : 2 * c_two]
    total[nine : nine + nine // 2] = jnp.concatenate(
        [grad_two[: nine // 2, 2 * c_two :], grad_two[nine // 2 :, 2 * c_two :]], axis=1
    )

    wb = wb_ref[...]
    grad_one = None
    for i in range(Z):
        w, j = own + i, own + i - first_sg
        for q in range(Y // 2):
            lane = 2 * q * X
            taps = jnp.dot(wb, around(sg, j, lane + X, 2 * X, -1), preferred_element_type=F32)
            grad = (
                taps[c_one : 2 * c_one]
                + shift(taps[:c_one], -1, X)
                + shift(taps[2 * c_one :], 1, X)
            ).astype(BF16)
            back[i, :, lane : lane + 2 * X] = grad
            grad = grad.astype(F32) * 0.125
            for g in range(8):
                t = tan[w, g * c_one : (g + 1) * c_one, lane : lane + 2 * X]
                slope = (LEAK + 1.0) / 2 + ((1.0 - LEAK) / 2) * t
                first[g * c_one : (g + 1) * c_one, lane : lane + 2 * X] = (slope * grad).astype(BF16)
        row0 = pl.multiple_of(w * 16 * quarter, 8 * quarter)
        term = lax.dot_general(
            fine[pl.ds(row0, 32 * quarter), 2 * X : (2 + Y) * X],
            first[...],
            (((1,), (1,)), ((), ())),
            preferred_element_type=F32,
        )
        grad_one = term if grad_one is None else grad_one + term
    half = 4 * c_one
    third = 8 * quarter
    folded = grad_one[: 3 * third, :half] + grad_one[third:, half:]
    at = nine + nine // 2
    low = lax.broadcasted_iota(jnp.int32, (quarter, half), 1) < half // 2
    place = {1: 0, 2: 1, 3: 2, 0: 3}

    def piece(dz, s, fy):
        row = dz * third + (s * 4 + place[fy]) * quarter
        return folded[row : row + quarter]

    for dz in range(3):
        for dy in range(3):
            left = piece(dz, 0, dy) + pltpu.roll(piece(dz, 0, dy + 1), half // 2, 1)
            right = pltpu.roll(piece(dz, 1, dy), half // 2, 1) + piece(dz, 1, dy + 1)
            total[at : at + quarter] = jnp.where(low, left, right)
            at += quarter
    if at < total.shape[0]:
        total[at:] = jnp.zeros((total.shape[0] - at, total.shape[1]), F32)
    rows = total.shape[0] // 2
    keep_ref[...] = total[pl.ds(pl.multiple_of(me * rows, rows), rows)]
    give_ref[...] = total[pl.ds(pl.multiple_of((1 - me) * rows, rows), rows)]

    for i in range(Z):
        lines = [act[own + i + 1, :, (2 + y) * X : (3 + y) * X] for y in range(Y)]
        lines = jnp.stack([line.astype(F32) for line in lines])
        out_ref[0, :, i] = jnp.swapaxes(lines, 0, 1).astype(BF16)
        lines = [back[i, :, y * X : (y + 1) * X] for y in range(Y)]
        lines = jnp.stack([line.astype(F32) for line in lines])
        out_ref[1, :, i] = jnp.swapaxes(lines, 0, 1).astype(BF16)


def join_kernel(own_ref, other_ref, act_ref, back_ref):
    me = lax.axis_index("pipe")
    act_ref[me] = own_ref[0]
    act_ref[1 - me] = other_ref[0]
    back_ref[me] = own_ref[1]
    back_ref[1 - me] = other_ref[1]


def unpack_kernel(plan, batch, own_ref, other_ref, one_ref, two_ref, full):
    c_in, c_one, c_two = plan.c_in, plan.c_one, plan.c_two
    me = lax.axis_index("pipe")
    rows = own_ref.shape[0]
    full[pl.ds(pl.multiple_of(me * rows, rows), rows)] = own_ref[...] * (1.0 / batch)
    full[pl.ds(pl.multiple_of((1 - me) * rows, rows), rows)] = other_ref[...] * (1.0 / batch)
    nine = 9 * c_one
    for zy in range(9):
        block = full[zy * c_one : (zy + 1) * c_one]
        two_ref[zy * 3] = block[:, :c_two]
        two_ref[zy * 3 + 1] = block[:, c_two:]
    part = c_one // 2
    for p in range(18):
        at = nine + (p % 9) * part
        lane = (p // 9) * c_two
        two_ref[(p // 2) * 3 + 2, (p % 2) * part : (p % 2 + 1) * part] = full[
            at : at + part, lane : lane + c_two
        ]
    for zy in range(9):
        at = nine + nine // 2 + zy * 2 * c_in
        block = full[at : at + 2 * c_in]
        mid, side = block[:, : 2 * c_one], block[:, 2 * c_one :]
        up, down = slice(0, c_in), slice(c_in, 2 * c_in)
        left, right = slice(0, c_one), slice(c_one, 2 * c_one)
        one_ref[zy * 3] = side[down, left] + mid[up, right]
        one_ref[zy * 3 + 1] = mid[up, left] + mid[down, right]
        one_ref[zy * 3 + 2] = mid[down, left] + side[up, right]


def vmem(count):
    return [pl.BlockSpec(memory_space=pltpu.VMEM)] * count


def shape(dims, dtype):
    return jax.ShapeDtypeStruct(dims, dtype)


def per_device(volumes, conv_one, conv_two, cotangent):
    plan = Plan(volumes, cotangent, conv_one, conv_two)
    X, Y, Z = plan.x, plan.y, plan.z
    c_in, c_one, c_two = plan.c_in, plan.c_one, plan.c_two
    keys = sorted({message_key(plan, k) for k in plan.kinds}, key=str)
    sent = pl.pallas_call(
        functools.partial(pack_kernel, plan, keys),
        out_shape=[shape((plan.rows(k), X), BF16) for k in keys],
        in_specs=vmem(2),
        out_specs=vmem(len(keys)),
        scratch_shapes=[
            pltpu.VMEM((Z, Y, plan.fold, X), BF16),
            pltpu.VMEM((plan.cz, plan.cy // 2, c_two, X), BF16),
        ],
        compiler_params=PARAMS,
        name="pack",
    )(volumes, cotangent)
    sent = dict(zip(keys, sent))
    msgs = []
    for kind in plan.kinds:
        cells = sent[message_key(plan, kind)]
        if kind != (None, None):
            z_pairs = None if kind[0] is None else pairs(plan.gz, kind[0])
            y_pairs = None if kind[1] is None else pairs(plan.gy, kind[1])
            cells = swap(cells, plan.gz, plan.gy, z_pairs, y_pairs)
        msgs.append(cells)

    w1, w2, wb = pl.pallas_call(
        functools.partial(weight_kernel, plan),
        out_shape=[
            shape((8 * c_one, 64 * c_in), BF16),
            shape((3 * c_two, 9 * c_one), BF16),
            shape((3 * c_one, 9 * c_two), BF16),
        ],
        in_specs=vmem(2),
        out_specs=vmem(3),
        compiler_params=PARAMS,
        cost_estimate=pl.CostEstimate(flops=10**7, bytes_accessed=10**6, transcendentals=0),
        name="weights",
    )(
        conv_one.transpose(2, 3, 4, 1, 0).reshape(27, c_in, c_one),
        conv_two.transpose(2, 3, 4, 1, 0).reshape(27, c_one, c_two),
    )

    used = 9 * c_one + 9 * c_one // 2 + 9 * 2 * c_in
    half_rows = -(-used // 32) * 16
    wide = 2 * c_two
    out, keep, give = pl.pallas_call(
        functools.partial(main_kernel, plan, len(msgs)),
        out_shape=[
            shape((2, c_one, Z, Y, X), BF16),
            shape((half_rows, wide), F32),
            shape((half_rows, wide), F32),
        ],
        in_specs=vmem(len(msgs) + 3),
        out_specs=vmem(3),
        scratch_shapes=[
            pltpu.VMEM((plan.win, plan.wide, plan.fold, X), BF16),
            pltpu.VMEM(((plan.win + 1) * 32 * c_in, plan.mid * X), BF16),
            pltpu.VMEM((plan.win + 2, c_one, plan.mid * X), BF16),
            pltpu.VMEM((plan.planes + 2, c_two, plan.slim * X), BF16),
            pltpu.VMEM((plan.cz + 2, c_two, plan.slim * X), BF16),
            pltpu.VMEM((plan.win, 8 * c_one, Y * X), F32),
            pltpu.VMEM((Z, c_one, Y * X), BF16),
            pltpu.VMEM((8 * c_one, Y * X), BF16),
            pltpu.VMEM((3 * c_two, Y * X), BF16),
            pltpu.VMEM((2 * half_rows, wide), F32),
        ],
        compiler_params=PARAMS,
        name="sections",
    )(*msgs, w1, w2, wb)

    both = pairs(lax.axis_size("pipe"), 0)
    other = lax.ppermute(out, "pipe", both)
    part = keep + lax.ppermute(give, "pipe", both)
    for axis in ("dp", "gz", "gy"):
        step = 1
        while step < lax.axis_size(axis):
            perm = [(i, i ^ step) for i in range(lax.axis_size(axis))]
            part = part + lax.ppermute(part, axis, perm)
            step *= 2
    rest = lax.ppermute(part, "pipe", both)
    size = (2, c_one, Z, Y, X)
    all_act, all_back = pl.pallas_call(
        join_kernel,
        out_shape=[shape(size, BF16)] * 2,
        in_specs=vmem(2),
        out_specs=vmem(2),
        compiler_params=PARAMS,
        name="join",
    )(out, other)
    grad_one, grad_two = pl.pallas_call(
        functools.partial(unpack_kernel, plan, volumes.shape[0] * lax.axis_size("dp")),
        out_shape=[shape((27, c_in, c_one), F32), shape((27, c_one, c_two), F32)],
        in_specs=vmem(2),
        out_specs=vmem(2),
        scratch_shapes=[pltpu.VMEM((2 * half_rows, wide), F32)],
        compiler_params=PARAMS,
        name="unpack",
    )(part, rest)
    grad_one = grad_one.reshape(3, 3, 3, c_in, c_one).transpose(4, 3, 0, 1, 2)
    grad_two = grad_two.reshape(3, 3, 3, c_one, c_two).transpose(4, 3, 0, 1, 2)
    return all_act, all_back, grad_one, grad_two


def solution(mesh):
    in_specs = (P("dp", None, "gz", "gy", None), P(), P(), P("dp", None, "gz", "gy", None))
    out_specs = (P("dp", None, "gz", "gy", None), P("dp", None, "gz", "gy", None), P(), P())
    return jax.shard_map(
        per_device, mesh=mesh, in_specs=in_specs, out_specs=out_specs, check_vma=False
    )
```

```python
import functools

import jax
import jax.numpy as jnp
from jax import lax
from jax.experimental import pallas as pl
from jax.experimental.pallas import tpu as pltpu
from jax.sharding import PartitionSpec as P

LEAK = 0.3
REACH = 3
AXES = ("dp", "pipe", "gz", "gy")
F32 = jnp.float32
BF16 = jnp.bfloat16
PARAMS = pltpu.CompilerParams(vmem_limit_bytes=48 * 1024 * 1024)


def pairs(count, odd):
    out = []
    for i in range(odd, count - 1, 2):
        out += [(i, i + 1), (i + 1, i)]
    return out


def swap(cells, plan, kind):
    z_kind, y_kind = kind
    if plan.split:
        perm = []
        for d in range(plan.dp):
            for p in range(2):
                for a in range(plan.gz):
                    for c in range(plan.gy):
                        to = [d, p, a if z_kind is None else 1 - a, c]
                        if y_kind is not None:
                            near = c + 2 * p - 1
                            if 0 <= near < plan.gy:
                                to[1], to[3] = 1 - p, near
                            else:
                                to = [d ^ 1 if d ^ 1 < plan.dp else d, p, a, c]
                        perm.append((plan.index(d, p, a, c), plan.index(*to)))
        return lax.ppermute(cells, AXES, perm)
    z_list = [(i, i) for i in range(plan.gz)] if z_kind is None else pairs(plan.gz, z_kind)
    y_list = [(i, i) for i in range(plan.gy)] if y_kind is None else pairs(plan.gy, y_kind)
    perm = [(a * plan.gy + c, b * plan.gy + d) for a, b in z_list for c, d in y_list]
    return lax.ppermute(cells, ("gz", "gy"), perm)


def shift(block, step, width):
    parts = []
    for at in range(0, block.shape[1], width):
        part = block[:, at : at + width]
        lane = lax.broadcasted_iota(jnp.int32, part.shape, 1)
        edge = 0 if step > 0 else width - 1
        parts.append(jnp.where(lane == edge, 0.0, pltpu.roll(part, step % width, 1)))
    return parts[0] if len(parts) == 1 else jnp.concatenate(parts, axis=1)


class Plan:
    def __init__(self, volumes, cotangent, conv_one, conv_two):
        count, self.fold, self.z, self.y, self.x = volumes.shape
        self.c_one, self.c_in = conv_one.shape[:2]
        self.c_two = conv_two.shape[0]
        self.cz, self.cy = cotangent.shape[2:4]
        self.dp, self.pipe = lax.axis_size("dp"), lax.axis_size("pipe")
        self.gz, self.gy = lax.axis_size("gz"), lax.axis_size("gy")
        self.batch = count * self.dp
        self.split = count == self.gz == self.pipe == 2 and self.y % 4 == 0 and self.y >= 2 * REACH
        self.h = min(REACH, self.z)
        sides = min(self.gz - 1, 2)
        if self.split:
            self.r, self.o = self.y // 2, 2 * self.z
            self.win = self.planes = self.o
            self.cot_planes = 2 * self.cz + 2
            self.kinds = [(None, None), (0, 0), (None, 0), (0, None)]
        else:
            self.r, self.o = self.y, self.z
            self.win = self.z + sides * self.h
            self.planes = self.z + sides
            self.cot_planes = self.cz + 2
            z_kinds = [None] + [k for k in (0, 1) if len(pairs(self.gz, k)) > 0]
            y_kinds = [None] + [k for k in (0, 1) if len(pairs(self.gy, k)) > 0]
            self.kinds = [(a, b) for a in z_kinds for b in y_kinds]
        self.wide = self.r + 2 * REACH
        self.mid = self.r + 4
        self.slim = self.r + 2

    def index(self, d, p, a, c):
        return ((d * self.pipe + p) * self.gz + a) * self.gy + c

    def at_z(self):
        if self.split or self.gz == 1:
            return 0, 0
        if self.gz > 2:
            return self.h, self.h - 1
        me = lax.axis_index("gz")
        return me * self.h, me * (self.h - 1)

    def row0(self):
        return lax.axis_index("pipe") * self.r if self.split else 0

    def blocks(self, kind):
        z_kind, y_kind = kind
        nz, nc = (self.z, self.cz) if z_kind is None or self.split else (self.h, 1)
        ny, np_ = (self.y, self.cy // 2) if y_kind is None else (REACH, 1)
        return nz, ny, nc, np_

    def rows(self, kind):
        nz, ny, nc, np_ = self.blocks(kind)
        return nz * ny * self.fold + nc * np_ * self.c_two


def message_key(plan, kind):
    z_kind, y_kind = kind
    if not plan.split and z_kind is not None and plan.h == plan.z and plan.cz == 1:
        z_kind = None
    return z_kind, y_kind


def pack_kernel(plan, keys, vol_hbm, cot_hbm, *refs):
    out_refs, (vol_ref, cot_ref, cells, cots, sems) = refs[: len(keys)], refs[len(keys) :]
    count = vol_ref.shape[0]
    me, my_z, my_y = lax.axis_index("pipe"), lax.axis_index("gz"), lax.axis_index("gy")
    first = 0 if plan.split else me
    loads = [
        pltpu.make_async_copy(vol_hbm.at[pl.ds(first, count)], vol_ref, sems.at[0]),
        pltpu.make_async_copy(cot_hbm.at[pl.ds(first, count)], cot_ref, sems.at[1]),
    ]
    for load in loads:
        load.start()
    loads[0].wait()
    for v in range(count):
        for z in range(plan.z):
            block = jnp.swapaxes(vol_ref[v, :, z].astype(F32), 0, 1).astype(BF16)
            for y in range(plan.y):
                cells[v, z, y] = block[y]
    loads[1].wait()
    for v in range(count):
        for z in range(plan.cz):
            block = jnp.swapaxes(cot_ref[v, :, z].astype(F32), 0, 1)
            for m in range(plan.cy // 2):
                pair = jnp.concatenate([block[2 * m], block[2 * m + 1]], axis=1)
                cots[v, z, m] = pair.astype(BF16)
    for key, out_ref in zip(keys, out_refs):
        nz, ny, nc, np_ = plan.blocks(key)
        v = z0 = c0 = y0 = p0 = 0
        if plan.split:
            v = my_z if key[0] is None else 1 - my_z
            y_low = me == 0
        else:
            if key[0] is not None:
                z_low = my_z % 2 == 1 - key[0]
                z0 = jnp.where(z_low, 0, plan.z - nz)
                c0 = jnp.where(z_low, 0, plan.cz - nc)
            if key[1] is not None:
                y_low = my_y % 2 == 1 - key[1]
        if key[1] is not None:
            y0 = jnp.where(y_low, 0, plan.y - ny)
            p0 = jnp.where(y_low, 0, plan.cy // 2 - np_)
        at = 0
        for i in range(nz):
            for j in range(ny):
                out_ref[at : at + plan.fold] = cells[v, z0 + i, y0 + j]
                at += plan.fold
        for i in range(nc):
            for j in range(np_):
                out_ref[at : at + plan.c_two] = cots[v, c0 + i, p0 + j]
                at += plan.c_two


def weight_kernel(plan, one_ref, two_ref, w1_ref, w2_ref, wb_ref):
    c_in, c_one, c_two = plan.c_in, plan.c_one, plan.c_two
    none = jnp.zeros((c_in, c_one), F32)
    pairs_x = {}
    for dz in range(3):
        for dy in range(3):
            tap = [one_ref[(dz * 3 + dy) * 3 + dx].astype(F32) * 0.5 for dx in range(3)]
            pairs_x[dz, dy, 0] = jnp.concatenate(
                [jnp.concatenate([tap[1], tap[0]], 1), jnp.concatenate([tap[2], tap[1]], 1)], 0
            )
            pairs_x[dz, dy, 1] = jnp.concatenate(
                [jnp.concatenate([none, tap[2]], 1), jnp.concatenate([tap[0], none], 1)], 0
            )
    blank = jnp.zeros((2 * c_in, 2 * c_one), F32)
    rows = []
    for fz in range(4):
        for s in range(2):
            for fy in (1, 2, 3, 0):
                rows.append(
                    jnp.concatenate(
                        [
                            pairs_x.get((fz - a, fy - b, s), blank)
                            for a in range(2)
                            for b in range(2)
                        ],
                        axis=1,
                    )
                )
    w1_ref[...] = jnp.concatenate(rows, axis=0).T.astype(BF16)
    for dx in range(3):
        taps = [two_ref[zy * 3 + dx] for zy in range(9)]
        wb_ref[dx * c_one : (dx + 1) * c_one] = jnp.concatenate(taps, axis=1)
        tall = jnp.concatenate([t.astype(F32) * 0.5 for t in taps], axis=0)
        w2_ref[dx * c_two : (dx + 1) * c_two] = tall.T.astype(BF16)


def around(ref, w, lane, size, step, sign):
    return jnp.concatenate(
        [
            ref[w + 1 + sign * dz, :, lane + sign * dy * step : lane + sign * dy * step + size]
            for dz in (-1, 0, 1)
            for dy in (-1, 0, 1)
        ],
        axis=0,
    )


def forward_kernel(plan, count, *refs):
    msgs = refs[:count]
    w1_ref, w2_ref, keep_ref, give_ref, fine, act, sg, tan = refs[count : count + 8]
    cells, cot, sgx, total = refs[count + 8 :]
    X, Y, Z, R = plan.x, plan.y, plan.z, plan.r
    fold, c_in, c_one, c_two = plan.fold, plan.c_in, plan.c_one, plan.c_two
    me, my_z, my_y = lax.axis_index("pipe"), lax.axis_index("gz"), lax.axis_index("gy")
    own, first_sg = plan.at_z()
    row0 = plan.row0()
    low_ok, high_ok = my_y > 0, my_y < plan.gy - 1
    if plan.split:
        low_ok, high_ok = low_ok | (me == 1), high_ok | (me == 0)

    pick = (
        lax.broadcasted_iota(jnp.int32, (X, 2 * X), 1) // 2
        == lax.broadcasted_iota(jnp.int32, (X, 2 * X), 0)
    )
    pick = jnp.where(pick, 0.125, 0.0).astype(BF16)
    if not plan.split:
        cot[...] = jnp.zeros_like(cot)
    for kind, msg in zip(plan.kinds, msgs):
        nz, ny, nc, np_ = plan.blocks(kind)
        z_kind, y_kind = kind
        below, used = None, None
        if plan.split:
            half = my_z if z_kind is None else 1 - my_z
            z0, c0 = half * Z, half * plan.cz + 1
            if y_kind is not None:
                below = me == 0
                used = (below & (my_y > 0)) | ((me == 1) & (my_y < plan.gy - 1))
        else:
            z0, c0 = own, 1
            if z_kind is not None:
                before = my_z % 2 == 1 - z_kind
                z0 = jnp.clip(jnp.where(before, own - plan.h, own + Z), 0, plan.win - plan.h)
                c0 = jnp.where(before, 0, plan.cz + 1)
            if y_kind is not None:
                below = my_y % 2 == 1 - y_kind
        y0 = REACH if y_kind is None else jnp.where(below, 0, Y + REACH)
        at = 0
        for i in range(nz):
            for j in range(ny):
                block = msg[at : at + fold]
                if used is not None:
                    block = jnp.where(used, block, jnp.zeros_like(block))
                cells[z0 + i, y0 + j] = block
                at += fold
        for i in range(nc):
            for j in range(np_):
                up = jnp.dot(msg[at : at + c_two], pick, preferred_element_type=F32)
                if used is not None:
                    up = jnp.where(used, up, 0.0)
                up = up.astype(BF16)
                at += c_two
                one, two = up[:, :X], up[:, X:]
                if y_kind is None:
                    for r, piece in enumerate((one, one, two, two)):
                        lane = (4 * j + r + 2) * X
                        cot[c0 + i, :, lane : lane + X] = piece
                else:
                    piece = jnp.where(below, two, one)
                    lane = pl.multiple_of(jnp.where(below, X, (Y + 2) * X), X)
                    cot[c0 + i, :, pl.ds(lane, X)] = piece

    quarter = 2 * c_in
    fine[0 : 8 * quarter] = jnp.zeros((8 * quarter, plan.mid * X), BF16)
    last = 8 * quarter + plan.win * 16 * quarter
    fine[last : last + 8 * quarter] = jnp.zeros((8 * quarter, plan.mid * X), BF16)
    is_c = (lax.broadcasted_iota(jnp.int32, (fold, X), 0) // c_in) % 2 == 1

    def spread(w, carry):
        base = pl.multiple_of(8 * quarter + w * 16 * quarter, 8 * quarter)
        kept = []
        for r in range(plan.wide):
            mid = cells[w, row0 + r].astype(F32)
            side = jnp.where(is_c, shift(mid, 1, X), shift(mid, -1, X))
            kept.append((mid, side))
            if r < 2:
                continue
            lane = (r - 2) * X
            for a in range(2):
                for s in range(2):
                    lo, here, hi = kept[r - 2][s], kept[r - 1][s], kept[r][s]
                    at = a * 2 * quarter
                    near = here[at : at + 2 * quarter]
                    far = jnp.concatenate(
                        [hi[at : at + quarter], lo[at + quarter : at + 2 * quarter]], axis=0
                    )
                    row = base + (a * 8 + s * 4) * quarter
                    fine[pl.ds(row, 2 * quarter), lane : lane + X] = near.astype(BF16)
                    fine[pl.ds(row + 2 * quarter, 2 * quarter), lane : lane + X] = far.astype(BF16)
        return carry

    lax.fori_loop(0, plan.win, spread, 0)

    w1 = w1_ref[...]
    last_q = plan.mid // 2 - 1
    act[0] = jnp.zeros(act.shape[1:], BF16)
    act[plan.win + 1] = jnp.zeros(act.shape[1:], BF16)

    def first_section(w, carry):
        top = pl.multiple_of(w * 16 * quarter, 8 * quarter)
        z_abs = my_z * Z + w - own
        z_ok = None if plan.split else (z_abs >= 0) & (z_abs < plan.gz * Z)
        for q in range(plan.mid // 2):
            lane = 2 * q * X
            half = jnp.dot(
                w1, fine[pl.ds(top, 32 * quarter), lane : lane + 2 * X], preferred_element_type=F32
            )
            line, prod = None, None
            for g in range(8):
                v = half[g * c_one : (g + 1) * c_one]
                t = jnp.tanh(v)
                if 0 < q < last_q:
                    tan[w, g * c_one : (g + 1) * c_one, lane - 2 * X : lane] = t
                bent = jnp.maximum(v, LEAK * v)
                grown = 1.0 + jnp.abs(t)
                line = bent if line is None else line + bent
                prod = grown if prod is None else prod * grown
            mean = 0.25 * line - ((1.0 - LEAK) / 8.0) * jnp.log(prod)
            for ok in (z_ok, low_ok if q == 0 else None, high_ok if q == last_q else None):
                if ok is not None:
                    mean = jnp.where(ok, mean, 0.0)
            act[w + 1, :, lane : lane + 2 * X] = mean.astype(BF16)
        return carry

    lax.fori_loop(0, plan.win, first_section, 0)

    w2 = w2_ref[...]
    sg[0] = jnp.zeros(sg.shape[1:], BF16)
    sg[plan.planes + 1] = jnp.zeros(sg.shape[1:], BF16)

    def second_section(j, carry):
        w = first_sg + j
        c_at = (w - own + 2) // 2
        for q in range(plan.slim // 2):
            lane = 2 * q * X
            taps = jnp.dot(w2, around(act, w, lane + X, 2 * X, X, 1), preferred_element_type=F32)
            half = (
                taps[c_two : 2 * c_two]
                + shift(taps[:c_two], 1, X)
                + shift(taps[2 * c_two :], -1, X)
            )
            slope = (LEAK + 1.0) / 2 + ((1.0 - LEAK) / 2) * jnp.tanh(half)
            near = pl.multiple_of((row0 + 1) * X + lane, X)
            part = cot[c_at, :, pl.ds(near, 2 * X)].astype(F32)
            sg[j + 1, :, lane : lane + 2 * X] = (slope * part).astype(BF16)
        return carry

    lax.fori_loop(0, plan.planes, second_section, 0)

    grad_two = None
    for i in range(plan.o):
        w, j = own + i, own + i - first_sg
        for y in range(R):
            mid = sg[j + 1, :, (y + 1) * X : (y + 2) * X]
            wide = mid.astype(F32)
            at = slice(y * X, (y + 1) * X)
            sgx[0:c_two, at] = shift(wide, -1, X).astype(BF16)
            sgx[c_two : 2 * c_two, at] = mid
            sgx[2 * c_two : 3 * c_two, at] = shift(wide, 1, X).astype(BF16)
        term = lax.dot_general(
            around(act, w, 2 * X, R * X, X, 1),
            sgx[...],
            (((1,), (1,)), ((), ())),
            preferred_element_type=F32,
        )
        grad_two = term if grad_two is None else grad_two + term
    nine = 9 * c_one
    total[0:nine] = grad_two[:, : 2 * c_two]
    total[nine : nine + nine // 2] = jnp.concatenate(
        [grad_two[: nine // 2, 2 * c_two :], grad_two[nine // 2 :, 2 * c_two :]], axis=1
    )
    rest = total.shape[0] - nine - nine // 2
    if rest > 0:
        total[nine + nine // 2 :] = jnp.zeros((rest, total.shape[1]), F32)
    rows = total.shape[0] // 2
    keep_ref[...] = total[pl.ds(pl.multiple_of(me * rows, rows), rows)]
    give_ref[...] = total[pl.ds(pl.multiple_of((1 - me) * rows, rows), rows)].astype(BF16)


def backward_kernel(plan, wb_ref, fine, act, sg, tan, one_ref, *refs):
    out_refs, (back, first) = refs[:-2], refs[-2:]
    X, Z, R = plan.x, plan.z, plan.r
    c_in, c_one = plan.c_in, plan.c_one
    quarter = 2 * c_in
    own, first_sg = plan.at_z()
    wb = wb_ref[...]
    grad_one = None
    for i in range(plan.o):
        w, j = own + i, own + i - first_sg
        for q in range(R // 2):
            lane = 2 * q * X
            taps = jnp.dot(wb, around(sg, j, lane + X, 2 * X, X, -1), preferred_element_type=F32)
            grad = (
                taps[c_one : 2 * c_one]
                + shift(taps[:c_one], -1, X)
                + shift(taps[2 * c_one :], 1, X)
            ).astype(BF16)
            back[i, :, lane : lane + 2 * X] = grad
            grad = grad.astype(F32) * 0.125
            for g in range(8):
                t = tan[w, g * c_one : (g + 1) * c_one, lane : lane + 2 * X]
                slope = (LEAK + 1.0) / 2 + ((1.0 - LEAK) / 2) * t
                first[g * c_one : (g + 1) * c_one, lane : lane + 2 * X] = (slope * grad).astype(BF16)
        top = w * 16 * quarter
        if not isinstance(top, int):
            top = pl.multiple_of(top, 8 * quarter)
        term = lax.dot_general(
            fine[pl.ds(top, 32 * quarter), 2 * X : (2 + R) * X],
            first[...],
            (((1,), (1,)), ((), ())),
            preferred_element_type=F32,
        )
        grad_one = term if grad_one is None else grad_one + term
    half = 4 * c_one
    third = 8 * quarter
    folded = grad_one[: 3 * third, :half] + grad_one[third:, half:]
    place = {1: 0, 2: 1, 3: 2, 0: 3}

    def piece(dz, s, fy):
        row = dz * third + (s * 4 + place[fy]) * quarter
        return folded[row : row + quarter]

    taps = []
    up, down = slice(0, c_in), slice(c_in, 2 * c_in)
    left, right = slice(0, c_one), slice(c_one, 2 * c_one)
    for dz in range(3):
        for dy in range(3):
            mid, side = (
                piece(dz, s, dy)[:, : half // 2] + piece(dz, s, dy + 1)[:, half // 2 :]
                for s in range(2)
            )
            taps.append(side[down, left] + mid[up, right])
            taps.append(mid[up, left] + mid[down, right])
            taps.append(mid[down, left] + side[up, right])
    per = one_ref.shape[1] // c_one
    taps += [jnp.zeros((c_in, c_one), F32)] * (-len(taps) % (2 * per))
    for at in range(0, len(taps), 2 * per):
        pair = [jnp.concatenate(taps[at + k : at + k + per], axis=1) for k in (0, per)]
        row = at // per * c_in
        one_ref[row : row + 2 * c_in] = jnp.concatenate(pair, axis=0)
    done = len(taps) // per * c_in
    if done < one_ref.shape[0]:
        one_ref[done:] = jnp.zeros((one_ref.shape[0] - done, one_ref.shape[1]), F32)

    for k, out_ref in enumerate(out_refs):
        z0 = 0
        if plan.split:
            my_z = lax.axis_index("gz")
            z0 = (my_z if k == 0 else 1 - my_z) * Z
        for i in range(Z):
            for y in range(R):
                out_ref[0, i, y] = act[own + z0 + i + 1, :, (2 + y) * X : (3 + y) * X]
                out_ref[1, i, y] = back[z0 + i, :, y * X : (y + 1) * X]


def join_kernel(plan, *refs):
    parts, outs = refs[:-2], refs[-2:]
    me = lax.axis_index("pipe")
    my_z = lax.axis_index("gz")
    for i in range(plan.z):
        for kind, out_ref in enumerate(outs):
            if plan.split:
                mine, theirs, mine_far, theirs_far = parts
                for v, (here, far) in enumerate(((mine, mine_far), (theirs, theirs_far))):
                    one, two = here[kind, i].astype(F32), far[kind, i].astype(F32)
                    low, high = jnp.where(me == 0, one, two), jnp.where(me == 0, two, one)
                    lines = jnp.concatenate([low, high], axis=0)
                    at = my_z if v == 0 else 1 - my_z
                    out_ref[at, :, i] = jnp.swapaxes(lines, 0, 1).astype(BF16)
            else:
                for v, part in enumerate(parts):
                    at = me if v == 0 else 1 - me
                    lines = part[kind, i].astype(F32)
                    out_ref[at, :, i] = jnp.swapaxes(lines, 0, 1).astype(BF16)


def unpack_kernel(plan, own_ref, other_ref, one_ref, two_ref, full):
    c_in, c_one, c_two = plan.c_in, plan.c_one, plan.c_two
    me = lax.axis_index("pipe")
    rows = full.shape[0] // 2
    scale = 1.0 / plan.batch
    full[pl.ds(pl.multiple_of(me * rows, rows), rows)] = own_ref[:rows] * scale
    full[pl.ds(pl.multiple_of((1 - me) * rows, rows), rows)] = other_ref[:rows] * scale
    nine = 9 * c_one
    for zy in range(9):
        block = full[zy * c_one : (zy + 1) * c_one]
        two_ref[zy * 3] = block[:, :c_two]
        two_ref[zy * 3 + 1] = block[:, c_two:]
    part = c_one // 2
    for p in range(18):
        at = nine + (p % 9) * part
        lane = (p // 9) * c_two
        two_ref[(p // 2) * 3 + 2, (p % 2) * part : (p % 2 + 1) * part] = full[
            at : at + part, lane : lane + c_two
        ]
    ones = (own_ref[rows:] + other_ref[rows:]) * scale
    per = ones.shape[1] // c_one
    for t in range(27):
        row, lane = t // per * c_in, t % per * c_one
        one_ref[t] = ones[row : row + c_in, lane : lane + c_one]


def vmem(count):
    return [pl.BlockSpec(memory_space=pltpu.VMEM)] * count


def shape(dims, dtype):
    return jax.ShapeDtypeStruct(dims, dtype)


def bits(axis):
    return [(axis, 1 << k) for k in range((lax.axis_size(axis) - 1).bit_length())]


def partner(plan, part, moves):
    perm = []
    for d in range(plan.dp):
        for p in range(plan.pipe):
            for a in range(plan.gz):
                for c in range(plan.gy):
                    at = {"dp": d, "pipe": p, "gz": a, "gy": c}
                    to = dict(at)
                    for axis, step in moves:
                        to[axis] ^= step
                    perm.append((plan.index(d, p, a, c), plan.index(*to.values())))
    return lax.ppermute(part, AXES, perm)


def sum_replicas(plan, part):
    moves = bits("dp") + bits("gz") + bits("gy")
    while moves:
        first, moves = moves[0], moves[1:]
        sent = part.astype(BF16)
        part = sent.astype(F32) + partner(plan, sent, [first]).astype(F32)
        if moves:
            second, moves = moves[0], moves[1:]
            part = part + (
                partner(plan, sent, [second]).astype(F32)
                + partner(plan, sent, [first, second]).astype(F32)
            )
    return part


def per_device(volumes, conv_one, conv_two, cotangent):
    plan = Plan(volumes, cotangent, conv_one, conv_two)
    X, Y, Z, R = plan.x, plan.y, plan.z, plan.r
    c_in, c_one, c_two = plan.c_in, plan.c_one, plan.c_two
    keys = sorted({message_key(plan, k) for k in plan.kinds}, key=str)
    count = 2 if plan.split else 1
    sent = pl.pallas_call(
        functools.partial(pack_kernel, plan, keys),
        out_shape=[shape((plan.rows(k), X), BF16) for k in keys],
        in_specs=[pl.BlockSpec(memory_space=pltpu.HBM)] * 2,
        out_specs=vmem(len(keys)),
        scratch_shapes=[
            pltpu.VMEM((count,) + volumes.shape[1:], BF16),
            pltpu.VMEM((count,) + cotangent.shape[1:], BF16),
            pltpu.VMEM((count, Z, Y, plan.fold, X), BF16),
            pltpu.VMEM((count, plan.cz, plan.cy // 2, c_two, X), BF16),
            pltpu.SemaphoreType.DMA((2,)),
        ],
        compiler_params=PARAMS,
        name="pack",
    )(volumes, cotangent)
    sent = dict(zip(keys, sent))
    msgs = []
    for kind in plan.kinds:
        cells = sent[message_key(plan, kind)]
        msgs.append(cells if kind == (None, None) else swap(cells, plan, kind))

    w1, w2, wb = pl.pallas_call(
        functools.partial(weight_kernel, plan),
        out_shape=[
            shape((8 * c_one, 64 * c_in), BF16),
            shape((3 * c_two, 9 * c_one), BF16),
            shape((3 * c_one, 9 * c_two), BF16),
        ],
        in_specs=vmem(2),
        out_specs=vmem(3),
        compiler_params=PARAMS,
        cost_estimate=pl.CostEstimate(flops=10**7, bytes_accessed=10**6, transcendentals=0),
        name="weights",
    )(
        conv_one.transpose(2, 3, 4, 1, 0).reshape(27, c_in, c_one),
        conv_two.transpose(2, 3, 4, 1, 0).reshape(27, c_one, c_two),
    )

    wide = 2 * c_two
    two_rows = -(-27 * c_one // 64) * 16
    one_rows = -(-27 * c_in * c_one // (16 * wide)) * 16
    keep, give, fine, act, sg, tan = pl.pallas_call(
        functools.partial(forward_kernel, plan, len(msgs)),
        out_shape=[
            shape((two_rows, wide), F32),
            shape((two_rows, wide), BF16),
            shape(((plan.win + 1) * 32 * c_in, plan.mid * X), BF16),
            shape((plan.win + 2, c_one, plan.mid * X), BF16),
            shape((plan.planes + 2, c_two, plan.slim * X), BF16),
            shape((plan.win, 8 * c_one, R * X), F32),
        ],
        in_specs=vmem(len(msgs) + 2),
        out_specs=vmem(6),
        scratch_shapes=[
            pltpu.VMEM((plan.win, Y + 2 * REACH, plan.fold, X), BF16),
            pltpu.VMEM((plan.cot_planes, c_two, (Y + 4) * X), BF16),
            pltpu.VMEM((3 * c_two, R * X), BF16),
            pltpu.VMEM((2 * two_rows, wide), F32),
        ],
        compiler_params=PARAMS,
        name="forward",
    )(*msgs, w1, w2)

    both = [("pipe", 1)]
    part = keep + partner(plan, give, both).astype(F32)
    blocks = shape((2, Z, R, c_one, X), BF16)
    one, *outs = pl.pallas_call(
        functools.partial(backward_kernel, plan),
        out_shape=[shape((one_rows, wide), F32)] + [blocks] * (2 if plan.split else 1),
        in_specs=vmem(5),
        out_specs=vmem(3 if plan.split else 2),
        scratch_shapes=[
            pltpu.VMEM((plan.o, c_one, R * X), BF16),
            pltpu.VMEM((8 * c_one, R * X), BF16),
        ],
        compiler_params=PARAMS,
        cost_estimate=pl.CostEstimate(flops=10**9, bytes_accessed=10**7, transcendentals=0),
        name="backward",
    )(wb, fine, act, sg, tan)

    part = sum_replicas(plan, jnp.concatenate([part, one], axis=0))
    rest = partner(plan, part, both)
    if plan.split:
        outs = [outs[0], partner(plan, outs[1], [("gz", 1)])]
    outs = outs + [partner(plan, out, both) for out in outs]
    size = (2, c_one, Z, Y, X)
    all_act, all_back = pl.pallas_call(
        functools.partial(join_kernel, plan),
        out_shape=[shape(size, BF16)] * 2,
        in_specs=vmem(len(outs)),
        out_specs=vmem(2),
        compiler_params=PARAMS,
        name="join",
    )(*outs)
    grad_one, grad_two = pl.pallas_call(
        functools.partial(unpack_kernel, plan),
        out_shape=[shape((27, c_in, c_one), F32), shape((27, c_one, c_two), F32)],
        in_specs=vmem(2),
        out_specs=vmem(2),
        scratch_shapes=[pltpu.VMEM((2 * two_rows, wide), F32)],
        compiler_params=PARAMS,
        name="unpack",
    )(part, rest)
    grad_one = grad_one.reshape(3, 3, 3, c_in, c_one).transpose(4, 3, 0, 1, 2)
    grad_two = grad_two.reshape(3, 3, 3, c_one, c_two).transpose(4, 3, 0, 1, 2)
    return all_act, all_back, grad_one, grad_two


def solution(mesh):
    in_specs = (P("dp", None, "gz", "gy", None), P(), P(), P("dp", None, "gz", "gy", None))
    out_specs = (P("dp", None, "gz", "gy", None), P("dp", None, "gz", "gy", None), P(), P())
    return jax.shard_map(
        per_device, mesh=mesh, in_specs=in_specs, out_specs=out_specs, check_vma=False
    )
```

```python
import functools

import jax
import jax.numpy as jnp
from jax import lax
from jax.experimental import pallas as pl
from jax.experimental.pallas import tpu as pltpu
from jax.sharding import PartitionSpec as P

LEAK = 0.3
REACH = 3
AXES = ("dp", "pipe", "gz", "gy")
F32 = jnp.float32
BF16 = jnp.bfloat16
PARAMS = pltpu.CompilerParams(vmem_limit_bytes=48 * 1024 * 1024)


def pairs(count, odd):
    out = []
    for i in range(odd, count - 1, 2):
        out += [(i, i + 1), (i + 1, i)]
    return out


def swap(cells, plan, kind):
    z_kind, y_kind = kind
    if plan.split:
        perm = []
        for d in range(plan.dp):
            for p in range(2):
                for a in range(plan.gz):
                    for c in range(plan.gy):
                        to = [d, p, a if z_kind is None else 1 - a, c]
                        if y_kind is not None:
                            near = c + 2 * p - 1
                            if 0 <= near < plan.gy:
                                to[1], to[3] = 1 - p, near
                            else:
                                to = [d ^ 1 if d ^ 1 < plan.dp else d, p, a, c]
                        perm.append((plan.index(d, p, a, c), plan.index(*to)))
        return lax.ppermute(cells, AXES, perm)
    z_list = [(i, i) for i in range(plan.gz)] if z_kind is None else pairs(plan.gz, z_kind)
    y_list = [(i, i) for i in range(plan.gy)] if y_kind is None else pairs(plan.gy, y_kind)
    perm = [(a * plan.gy + c, b * plan.gy + d) for a, b in z_list for c, d in y_list]
    return lax.ppermute(cells, ("gz", "gy"), perm)


def shift(block, step, width):
    parts = []
    for at in range(0, block.shape[1], width):
        part = block[:, at : at + width]
        lane = lax.broadcasted_iota(jnp.int32, part.shape, 1)
        edge = 0 if step > 0 else width - 1
        parts.append(jnp.where(lane == edge, 0.0, pltpu.roll(part, step % width, 1)))
    return parts[0] if len(parts) == 1 else jnp.concatenate(parts, axis=1)


class Plan:
    def __init__(self, volumes, cotangent, conv_one, conv_two):
        count, self.fold, self.z, self.y, self.x = volumes.shape
        self.c_one, self.c_in = conv_one.shape[:2]
        self.c_two = conv_two.shape[0]
        self.cz, self.cy = cotangent.shape[2:4]
        self.dp, self.pipe = lax.axis_size("dp"), lax.axis_size("pipe")
        self.gz, self.gy = lax.axis_size("gz"), lax.axis_size("gy")
        self.batch = count * self.dp
        self.split = count == self.gz == self.pipe == 2 and self.y % 4 == 0 and self.y >= 2 * REACH
        self.h = min(REACH, self.z)
        sides = min(self.gz - 1, 2)
        if self.split:
            self.r, self.o = self.y // 2, 2 * self.z
            self.win = self.planes = self.o
            self.cot_planes = 2 * self.cz + 2
            self.kinds = [(None, None), (0, 0), (None, 0), (0, None)]
        else:
            self.r, self.o = self.y, self.z
            self.win = self.z + sides * self.h
            self.planes = self.z + sides
            self.cot_planes = self.cz + 2
            z_kinds = [None] + [k for k in (0, 1) if len(pairs(self.gz, k)) > 0]
            y_kinds = [None] + [k for k in (0, 1) if len(pairs(self.gy, k)) > 0]
            self.kinds = [(a, b) for a in z_kinds for b in y_kinds]
        self.wide = self.r + 2 * REACH
        self.mid = self.r + 4
        self.slim = self.r + 2

    def index(self, d, p, a, c):
        return ((d * self.pipe + p) * self.gz + a) * self.gy + c

    def at_z(self):
        if self.split or self.gz == 1:
            return 0, 0
        if self.gz > 2:
            return self.h, self.h - 1
        me = lax.axis_index("gz")
        return me * self.h, me * (self.h - 1)

    def row0(self):
        return lax.axis_index("pipe") * self.r if self.split else 0

    def blocks(self, kind):
        z_kind, y_kind = kind
        nz, nc = (self.z, self.cz) if z_kind is None or self.split else (self.h, 1)
        ny, np_ = (self.y, self.cy // 2) if y_kind is None else (REACH, 1)
        return nz, ny, nc, np_

    def rows(self, kind):
        nz, ny, nc, np_ = self.blocks(kind)
        return nz * ny * self.fold + nc * np_ * self.c_two


def message_key(plan, kind):
    z_kind, y_kind = kind
    if not plan.split and z_kind is not None and plan.h == plan.z and plan.cz == 1:
        z_kind = None
    return z_kind, y_kind


def pack_kernel(plan, keys, vol_hbm, cot_hbm, *refs):
    out_refs, (vol_ref, cot_ref, cells, cots, sems) = refs[: len(keys)], refs[len(keys) :]
    count = vol_ref.shape[0]
    me, my_z, my_y = lax.axis_index("pipe"), lax.axis_index("gz"), lax.axis_index("gy")
    first = 0 if plan.split else me
    loads = [
        pltpu.make_async_copy(vol_hbm.at[pl.ds(first, count)], vol_ref, sems.at[0]),
        pltpu.make_async_copy(cot_hbm.at[pl.ds(first, count)], cot_ref, sems.at[1]),
    ]
    for load in loads:
        load.start()
    loads[0].wait()
    for v in range(count):
        for z in range(plan.z):
            block = jnp.swapaxes(vol_ref[v, :, z].astype(F32), 0, 1).astype(BF16)
            for y in range(plan.y):
                cells[v, z, y] = block[y]
    loads[1].wait()
    for v in range(count):
        for z in range(plan.cz):
            block = jnp.swapaxes(cot_ref[v, :, z].astype(F32), 0, 1)
            for m in range(plan.cy // 2):
                pair = jnp.concatenate([block[2 * m], block[2 * m + 1]], axis=1)
                cots[v, z, m] = pair.astype(BF16)
    for key, out_ref in zip(keys, out_refs):
        nz, ny, nc, np_ = plan.blocks(key)
        v = z0 = c0 = y0 = p0 = 0
        if plan.split:
            v = my_z if key[0] is None else 1 - my_z
            y_low = me == 0
        else:
            if key[0] is not None:
                z_low = my_z % 2 == 1 - key[0]
                z0 = jnp.where(z_low, 0, plan.z - nz)
                c0 = jnp.where(z_low, 0, plan.cz - nc)
            if key[1] is not None:
                y_low = my_y % 2 == 1 - key[1]
        if key[1] is not None:
            y0 = jnp.where(y_low, 0, plan.y - ny)
            p0 = jnp.where(y_low, 0, plan.cy // 2 - np_)
        at = 0
        for i in range(nz):
            for j in range(ny):
                out_ref[at : at + plan.fold] = cells[v, z0 + i, y0 + j]
                at += plan.fold
        for i in range(nc):
            for j in range(np_):
                out_ref[at : at + plan.c_two] = cots[v, c0 + i, p0 + j]
                at += plan.c_two


def weight_kernel(plan, one_ref, two_ref, w1_ref, w2_ref, wb_ref):
    c_in, c_one, c_two = plan.c_in, plan.c_one, plan.c_two
    none = jnp.zeros((c_in, c_one), F32)
    pairs_x = {}
    for dz in range(3):
        for dy in range(3):
            tap = [one_ref[(dz * 3 + dy) * 3 + dx].astype(F32) * 0.5 for dx in range(3)]
            pairs_x[dz, dy, 0] = jnp.concatenate(
                [jnp.concatenate([tap[1], tap[0]], 1), jnp.concatenate([tap[2], tap[1]], 1)], 0
            )
            pairs_x[dz, dy, 1] = jnp.concatenate(
                [jnp.concatenate([none, tap[2]], 1), jnp.concatenate([tap[0], none], 1)], 0
            )
    blank = jnp.zeros((2 * c_in, 2 * c_one), F32)
    rows = []
    for fz in range(4):
        for s in range(2):
            for fy in (1, 2, 3, 0):
                rows.append(
                    jnp.concatenate(
                        [
                            pairs_x.get((fz - a, fy - b, s), blank)
                            for a in range(2)
                            for b in range(2)
                        ],
                        axis=1,
                    )
                )
    w1_ref[...] = jnp.concatenate(rows, axis=0).T.astype(BF16)
    for dx in range(3):
        taps = [two_ref[zy * 3 + dx] for zy in range(9)]
        wb_ref[dx * c_one : (dx + 1) * c_one] = jnp.concatenate(taps, axis=1)
        tall = jnp.concatenate([t.astype(F32) * 0.5 for t in taps], axis=0)
        w2_ref[dx * c_two : (dx + 1) * c_two] = tall.T.astype(BF16)


def around(ref, w, lane, size, step, sign):
    return jnp.concatenate(
        [
            ref[w + 1 + sign * dz, :, lane + sign * dy * step : lane + sign * dy * step + size]
            for dz in (-1, 0, 1)
            for dy in (-1, 0, 1)
        ],
        axis=0,
    )


def forward_kernel(plan, count, *refs):
    msgs = refs[:count]
    w1_ref, w2_ref, keep_ref, give_ref, fine, act, sg, tan = refs[count : count + 8]
    cells, cot, sgx, total = refs[count + 8 :]
    X, Y, Z, R = plan.x, plan.y, plan.z, plan.r
    fold, c_in, c_one, c_two = plan.fold, plan.c_in, plan.c_one, plan.c_two
    me, my_z, my_y = lax.axis_index("pipe"), lax.axis_index("gz"), lax.axis_index("gy")
    own, first_sg = plan.at_z()
    row0 = plan.row0()
    low_ok, high_ok = my_y > 0, my_y < plan.gy - 1
    if plan.split:
        low_ok, high_ok = low_ok | (me == 1), high_ok | (me == 0)

    pick = (
        lax.broadcasted_iota(jnp.int32, (X, 2 * X), 1) // 2
        == lax.broadcasted_iota(jnp.int32, (X, 2 * X), 0)
    )
    pick = jnp.where(pick, 0.125, 0.0).astype(BF16)
    if not plan.split:
        cot[...] = jnp.zeros_like(cot)
    for kind, msg in zip(plan.kinds, msgs):
        nz, ny, nc, np_ = plan.blocks(kind)
        z_kind, y_kind = kind
        below, used = None, None
        if plan.split:
            half = my_z if z_kind is None else 1 - my_z
            z0, c0 = half * Z, half * plan.cz + 1
            if y_kind is not None:
                below = me == 0
                used = (below & (my_y > 0)) | ((me == 1) & (my_y < plan.gy - 1))
        else:
            z0, c0 = own, 1
            if z_kind is not None:
                before = my_z % 2 == 1 - z_kind
                z0 = jnp.clip(jnp.where(before, own - plan.h, own + Z), 0, plan.win - plan.h)
                c0 = jnp.where(before, 0, plan.cz + 1)
            if y_kind is not None:
                below = my_y % 2 == 1 - y_kind
        y0 = REACH if y_kind is None else jnp.where(below, 0, Y + REACH)
        at = 0
        for i in range(nz):
            for j in range(ny):
                block = msg[at : at + fold]
                if used is not None:
                    block = jnp.where(used, block, jnp.zeros_like(block))
                cells[z0 + i, y0 + j] = block
                at += fold
        for i in range(nc):
            for j in range(np_):
                up = jnp.dot(msg[at : at + c_two], pick, preferred_element_type=F32)
                if used is not None:
                    up = jnp.where(used, up, 0.0)
                up = up.astype(BF16)
                at += c_two
                one, two = up[:, :X], up[:, X:]
                if y_kind is None:
                    for r, piece in enumerate((one, one, two, two)):
                        lane = (4 * j + r + 2) * X
                        cot[c0 + i, :, lane : lane + X] = piece
                else:
                    piece = jnp.where(below, two, one)
                    lane = pl.multiple_of(jnp.where(below, X, (Y + 2) * X), X)
                    cot[c0 + i, :, pl.ds(lane, X)] = piece

    quarter = 2 * c_in
    fine[0 : 8 * quarter] = jnp.zeros((8 * quarter, plan.mid * X), BF16)
    last = 8 * quarter + plan.win * 16 * quarter
    fine[last : last + 8 * quarter] = jnp.zeros((8 * quarter, plan.mid * X), BF16)
    is_c = (lax.broadcasted_iota(jnp.int32, (fold, X), 0) // c_in) % 2 == 1

    def spread(w, carry):
        base = pl.multiple_of(8 * quarter + w * 16 * quarter, 8 * quarter)
        kept = []
        for r in range(plan.wide):
            mid = cells[w, row0 + r].astype(F32)
            side = jnp.where(is_c, shift(mid, 1, X), shift(mid, -1, X))
            kept.append((mid, side))
            if r < 2:
                continue
            lane = (r - 2) * X
            for a in range(2):
                for s in range(2):
                    lo, here, hi = kept[r - 2][s], kept[r - 1][s], kept[r][s]
                    at = a * 2 * quarter
                    near = here[at : at + 2 * quarter]
                    far = jnp.concatenate(
                        [hi[at : at + quarter], lo[at + quarter : at + 2 * quarter]], axis=0
                    )
                    row = base + (a * 8 + s * 4) * quarter
                    fine[pl.ds(row, 2 * quarter), lane : lane + X] = near.astype(BF16)
                    fine[pl.ds(row + 2 * quarter, 2 * quarter), lane : lane + X] = far.astype(BF16)
        return carry

    lax.fori_loop(0, plan.win, spread, 0, unroll=True)

    w1 = w1_ref[...]
    last_q = plan.mid // 2 - 1
    act[0] = jnp.zeros(act.shape[1:], BF16)
    act[plan.win + 1] = jnp.zeros(act.shape[1:], BF16)

    def first_section(w, carry):
        top = pl.multiple_of(w * 16 * quarter, 8 * quarter)
        z_abs = my_z * Z + w - own
        z_ok = None if plan.split else (z_abs >= 0) & (z_abs < plan.gz * Z)
        for q in range(plan.mid // 2):
            lane = 2 * q * X
            half = jnp.dot(
                w1, fine[pl.ds(top, 32 * quarter), lane : lane + 2 * X], preferred_element_type=F32
            )
            line, prod = None, None
            for g in range(8):
                v = half[g * c_one : (g + 1) * c_one]
                t = jnp.tanh(v)
                if 0 < q < last_q:
                    tan[w, g * c_one : (g + 1) * c_one, lane - 2 * X : lane] = t
                bent = jnp.maximum(v, LEAK * v)
                grown = 1.0 + jnp.abs(t)
                line = bent if line is None else line + bent
                prod = grown if prod is None else prod * grown
            mean = 0.25 * line - ((1.0 - LEAK) / 8.0) * jnp.log(prod)
            for ok in (z_ok, low_ok if q == 0 else None, high_ok if q == last_q else None):
                if ok is not None:
                    mean = jnp.where(ok, mean, 0.0)
            act[w + 1, :, lane : lane + 2 * X] = mean.astype(BF16)
        return carry

    lax.fori_loop(0, plan.win, first_section, 0, unroll=True)

    w2 = w2_ref[...]
    sg[0] = jnp.zeros(sg.shape[1:], BF16)
    sg[plan.planes + 1] = jnp.zeros(sg.shape[1:], BF16)

    def second_section(j, carry):
        w = first_sg + j
        c_at = (w - own + 2) // 2
        for q in range(plan.slim // 2):
            lane = 2 * q * X
            taps = jnp.dot(w2, around(act, w, lane + X, 2 * X, X, 1), preferred_element_type=F32)
            half = (
                taps[c_two : 2 * c_two]
                + shift(taps[:c_two], 1, X)
                + shift(taps[2 * c_two :], -1, X)
            )
            slope = (LEAK + 1.0) / 2 + ((1.0 - LEAK) / 2) * jnp.tanh(half)
            near = pl.multiple_of((row0 + 1) * X + lane, X)
            part = cot[c_at, :, pl.ds(near, 2 * X)].astype(F32)
            sg[j + 1, :, lane : lane + 2 * X] = (slope * part).astype(BF16)
        return carry

    lax.fori_loop(0, plan.planes, second_section, 0, unroll=True)

    grad_two = None
    for i in range(plan.o):
        w, j = own + i, own + i - first_sg
        for y in range(R):
            mid = sg[j + 1, :, (y + 1) * X : (y + 2) * X]
            wide = mid.astype(F32)
            at = slice(y * X, (y + 1) * X)
            sgx[0:c_two, at] = shift(wide, -1, X).astype(BF16)
            sgx[c_two : 2 * c_two, at] = mid
            sgx[2 * c_two : 3 * c_two, at] = shift(wide, 1, X).astype(BF16)
        term = lax.dot_general(
            around(act, w, 2 * X, R * X, X, 1),
            sgx[...],
            (((1,), (1,)), ((), ())),
            preferred_element_type=F32,
        )
        grad_two = term if grad_two is None else grad_two + term
    nine = 9 * c_one
    total[0:nine] = grad_two[:, : 2 * c_two]
    total[nine : nine + nine // 2] = jnp.concatenate(
        [grad_two[: nine // 2, 2 * c_two :], grad_two[nine // 2 :, 2 * c_two :]], axis=1
    )
    rest = total.shape[0] - nine - nine // 2
    if rest > 0:
        total[nine + nine // 2 :] = jnp.zeros((rest, total.shape[1]), F32)
    rows = total.shape[0] // 2
    keep_ref[...] = total[pl.ds(pl.multiple_of(me * rows, rows), rows)]
    give_ref[...] = total[pl.ds(pl.multiple_of((1 - me) * rows, rows), rows)].astype(BF16)


def backward_kernel(plan, wb_ref, fine, act, sg, tan, one_ref, *refs):
    out_refs, (back, first) = refs[:-2], refs[-2:]
    X, Z, R = plan.x, plan.z, plan.r
    c_in, c_one = plan.c_in, plan.c_one
    quarter = 2 * c_in
    own, first_sg = plan.at_z()
    wb = wb_ref[...]
    grad_one = None
    for i in range(plan.o):
        w, j = own + i, own + i - first_sg
        for q in range(R // 2):
            lane = 2 * q * X
            taps = jnp.dot(wb, around(sg, j, lane + X, 2 * X, X, -1), preferred_element_type=F32)
            grad = (
                taps[c_one : 2 * c_one]
                + shift(taps[:c_one], -1, X)
                + shift(taps[2 * c_one :], 1, X)
            ).astype(BF16)
            back[i, :, lane : lane + 2 * X] = grad
            grad = grad.astype(F32) * 0.125
            for g in range(8):
                t = tan[w, g * c_one : (g + 1) * c_one, lane : lane + 2 * X]
                slope = (LEAK + 1.0) / 2 + ((1.0 - LEAK) / 2) * t
                first[g * c_one : (g + 1) * c_one, lane : lane + 2 * X] = (slope * grad).astype(BF16)
        top = w * 16 * quarter
        if not isinstance(top, int):
            top = pl.multiple_of(top, 8 * quarter)
        term = lax.dot_general(
            fine[pl.ds(top, 32 * quarter), 2 * X : (2 + R) * X],
            first[...],
            (((1,), (1,)), ((), ())),
            preferred_element_type=F32,
        )
        grad_one = term if grad_one is None else grad_one + term
    half = 4 * c_one
    third = 8 * quarter
    folded = grad_one[: 3 * third, :half] + grad_one[third:, half:]
    place = {1: 0, 2: 1, 3: 2, 0: 3}

    def piece(dz, s, fy):
        row = dz * third + (s * 4 + place[fy]) * quarter
        return folded[row : row + quarter]

    taps = []
    up, down = slice(0, c_in), slice(c_in, 2 * c_in)
    left, right = slice(0, c_one), slice(c_one, 2 * c_one)
    for dz in range(3):
        for dy in range(3):
            mid, side = (
                piece(dz, s, dy)[:, : half // 2] + piece(dz, s, dy + 1)[:, half // 2 :]
                for s in range(2)
            )
            taps.append(side[down, left] + mid[up, right])
            taps.append(mid[up, left] + mid[down, right])
            taps.append(mid[down, left] + side[up, right])
    per = one_ref.shape[1] // c_one
    taps += [jnp.zeros((c_in, c_one), F32)] * (-len(taps) % (2 * per))
    for at in range(0, len(taps), 2 * per):
        pair = [jnp.concatenate(taps[at + k : at + k + per], axis=1) for k in (0, per)]
        row = at // per * c_in
        one_ref[row : row + 2 * c_in] = jnp.concatenate(pair, axis=0)
    done = len(taps) // per * c_in
    if done < one_ref.shape[0]:
        one_ref[done:] = jnp.zeros((one_ref.shape[0] - done, one_ref.shape[1]), F32)

    for k, out_ref in enumerate(out_refs):
        z0 = 0
        if plan.split:
            my_z = lax.axis_index("gz")
            z0 = (my_z if k == 0 else 1 - my_z) * Z
        for i in range(Z):
            for y in range(R):
                out_ref[0, i, y] = act[own + z0 + i + 1, :, (2 + y) * X : (3 + y) * X]
                out_ref[1, i, y] = back[z0 + i, :, y * X : (y + 1) * X]


def join_kernel(plan, *refs):
    parts, outs = refs[:-2], refs[-2:]
    me = lax.axis_index("pipe")
    my_z = lax.axis_index("gz")
    for i in range(plan.z):
        for kind, out_ref in enumerate(outs):
            if plan.split:
                mine, theirs, mine_far, theirs_far = parts
                for v, (here, far) in enumerate(((mine, mine_far), (theirs, theirs_far))):
                    one, two = here[kind, i].astype(F32), far[kind, i].astype(F32)
                    low, high = jnp.where(me == 0, one, two), jnp.where(me == 0, two, one)
                    lines = jnp.concatenate([low, high], axis=0)
                    at = my_z if v == 0 else 1 - my_z
                    out_ref[at, :, i] = jnp.swapaxes(lines, 0, 1).astype(BF16)
            else:
                for v, part in enumerate(parts):
                    at = me if v == 0 else 1 - me
                    lines = part[kind, i].astype(F32)
                    out_ref[at, :, i] = jnp.swapaxes(lines, 0, 1).astype(BF16)


def unpack_kernel(plan, own_ref, other_ref, one_ref, two_ref, full):
    c_in, c_one, c_two = plan.c_in, plan.c_one, plan.c_two
    me = lax.axis_index("pipe")
    rows = full.shape[0] // 2
    scale = 1.0 / plan.batch
    full[pl.ds(pl.multiple_of(me * rows, rows), rows)] = own_ref[:rows] * scale
    full[pl.ds(pl.multiple_of((1 - me) * rows, rows), rows)] = other_ref[:rows] * scale
    nine = 9 * c_one
    for zy in range(9):
        block = full[zy * c_one : (zy + 1) * c_one]
        two_ref[zy * 3] = block[:, :c_two]
        two_ref[zy * 3 + 1] = block[:, c_two:]
    part = c_one // 2
    for p in range(18):
        at = nine + (p % 9) * part
        lane = (p // 9) * c_two
        two_ref[(p // 2) * 3 + 2, (p % 2) * part : (p % 2 + 1) * part] = full[
            at : at + part, lane : lane + c_two
        ]
    ones = (own_ref[rows:] + other_ref[rows:]) * scale
    per = ones.shape[1] // c_one
    for t in range(27):
        row, lane = t // per * c_in, t % per * c_one
        one_ref[t] = ones[row : row + c_in, lane : lane + c_one]


def vmem(count):
    return [pl.BlockSpec(memory_space=pltpu.VMEM)] * count


def shape(dims, dtype):
    return jax.ShapeDtypeStruct(dims, dtype)


def bits(axis):
    return [(axis, 1 << k) for k in range((lax.axis_size(axis) - 1).bit_length())]


def partner(plan, part, moves, other_moves=None):
    perm = []
    for d in range(plan.dp):
        for p in range(plan.pipe):
            for a in range(plan.gz):
                for c in range(plan.gy):
                    to = {"dp": d, "pipe": p, "gz": a, "gy": c}
                    for axis, step in moves if p == 0 or other_moves is None else other_moves:
                        to[axis] ^= step
                    perm.append((plan.index(d, p, a, c), plan.index(*to.values())))
    return lax.ppermute(part, AXES, perm)


def sum_replicas(plan, part):
    moves = bits("dp") + bits("gz") + bits("gy")
    steps = [moves[i : i + 2] for i in range(0, len(moves), 2)]
    if any(len(step) == 1 for step in steps):
        orders = zip(steps, steps)
    else:
        orders = zip(steps[::-1], steps)
    for here, there in orders:
        sent = part.astype(BF16)
        got = [partner(plan, sent, here[:1], there[:1]).astype(F32)]
        if len(here) > 1:
            got.append(partner(plan, sent, here[1:], there[1:]).astype(F32))
            got.append(partner(plan, sent, here, there).astype(F32))
        part = sent.astype(F32) + got[0]
        if len(here) > 1:
            part = part + (got[1] + got[2])
    return part


def per_device(volumes, conv_one, conv_two, cotangent):
    plan = Plan(volumes, cotangent, conv_one, conv_two)
    X, Y, Z, R = plan.x, plan.y, plan.z, plan.r
    c_in, c_one, c_two = plan.c_in, plan.c_one, plan.c_two
    keys = sorted({message_key(plan, k) for k in plan.kinds}, key=str)
    count = 2 if plan.split else 1
    sent = pl.pallas_call(
        functools.partial(pack_kernel, plan, keys),
        out_shape=[shape((plan.rows(k), X), BF16) for k in keys],
        in_specs=[pl.BlockSpec(memory_space=pltpu.HBM)] * 2,
        out_specs=vmem(len(keys)),
        scratch_shapes=[
            pltpu.VMEM((count,) + volumes.shape[1:], BF16),
            pltpu.VMEM((count,) + cotangent.shape[1:], BF16),
            pltpu.VMEM((count, Z, Y, plan.fold, X), BF16),
            pltpu.VMEM((count, plan.cz, plan.cy // 2, c_two, X), BF16),
            pltpu.SemaphoreType.DMA((2,)),
        ],
        compiler_params=PARAMS,
        name="pack",
    )(*[pltpu.with_memory_space_constraint(a, pltpu.HBM) for a in (volumes, cotangent)])
    sent = dict(zip(keys, sent))
    msgs = []
    for kind in plan.kinds:
        cells = sent[message_key(plan, kind)]
        msgs.append(cells if kind == (None, None) else swap(cells, plan, kind))

    w1, w2, wb = pl.pallas_call(
        functools.partial(weight_kernel, plan),
        out_shape=[
            shape((8 * c_one, 64 * c_in), BF16),
            shape((3 * c_two, 9 * c_one), BF16),
            shape((3 * c_one, 9 * c_two), BF16),
        ],
        in_specs=vmem(2),
        out_specs=vmem(3),
        compiler_params=PARAMS,
        cost_estimate=pl.CostEstimate(flops=10**7, bytes_accessed=10**6, transcendentals=0),
        name="weights",
    )(
        conv_one.transpose(2, 3, 4, 1, 0).reshape(27, c_in, c_one),
        conv_two.transpose(2, 3, 4, 1, 0).reshape(27, c_one, c_two),
    )

    wide = 2 * c_two
    two_rows = -(-27 * c_one // 64) * 16
    one_rows = -(-27 * c_in * c_one // (16 * wide)) * 16
    keep, give, fine, act, sg, tan = pl.pallas_call(
        functools.partial(forward_kernel, plan, len(msgs)),
        out_shape=[
            shape((two_rows, wide), F32),
            shape((two_rows, wide), BF16),
            shape(((plan.win + 1) * 32 * c_in, plan.mid * X), BF16),
            shape((plan.win + 2, c_one, plan.mid * X), BF16),
            shape((plan.planes + 2, c_two, plan.slim * X), BF16),
            shape((plan.win, 8 * c_one, R * X), F32),
        ],
        in_specs=vmem(len(msgs) + 2),
        out_specs=vmem(6),
        scratch_shapes=[
            pltpu.VMEM((plan.win, Y + 2 * REACH, plan.fold, X), BF16),
            pltpu.VMEM((plan.cot_planes, c_two, (Y + 4) * X), BF16),
            pltpu.VMEM((3 * c_two, R * X), BF16),
            pltpu.VMEM((2 * two_rows, wide), F32),
        ],
        compiler_params=PARAMS,
        name="forward",
    )(*msgs, w1, w2)

    both = [("pipe", 1)]
    part = keep + partner(plan, give, both).astype(F32)
    blocks = shape((2, Z, R, c_one, X), BF16)
    one, *outs = pl.pallas_call(
        functools.partial(backward_kernel, plan),
        out_shape=[shape((one_rows, wide), F32)] + [blocks] * (2 if plan.split else 1),
        in_specs=vmem(5),
        out_specs=vmem(3 if plan.split else 2),
        scratch_shapes=[
            pltpu.VMEM((plan.o, c_one, R * X), BF16),
            pltpu.VMEM((8 * c_one, R * X), BF16),
        ],
        compiler_params=PARAMS,
        cost_estimate=pl.CostEstimate(flops=10**9, bytes_accessed=10**7, transcendentals=0),
        name="backward",
    )(wb, fine, act, sg, tan)

    part = sum_replicas(plan, jnp.concatenate([part, one], axis=0))
    rest = partner(plan, part, both)
    if plan.split:
        outs = [outs[0], partner(plan, outs[1], [("gz", 1)])]
    outs = outs + [partner(plan, out, both) for out in outs]
    size = (2, c_one, Z, Y, X)
    all_act, all_back = pl.pallas_call(
        functools.partial(join_kernel, plan),
        out_shape=[shape(size, BF16)] * 2,
        in_specs=vmem(len(outs)),
        out_specs=vmem(2),
        compiler_params=PARAMS,
        name="join",
    )(*outs)
    grad_one, grad_two = pl.pallas_call(
        functools.partial(unpack_kernel, plan),
        out_shape=[shape((27, c_in, c_one), F32), shape((27, c_one, c_two), F32)],
        in_specs=vmem(2),
        out_specs=vmem(2),
        scratch_shapes=[pltpu.VMEM((2 * two_rows, wide), F32)],
        compiler_params=PARAMS,
        name="unpack",
    )(part, rest)
    grad_one = grad_one.reshape(3, 3, 3, c_in, c_one).transpose(4, 3, 0, 1, 2)
    grad_two = grad_two.reshape(3, 3, 3, c_one, c_two).transpose(4, 3, 0, 1, 2)
    return all_act, all_back, grad_one, grad_two


def solution(mesh):
    in_specs = (P("dp", None, "gz", "gy", None), P(), P(), P("dp", None, "gz", "gy", None))
    out_specs = (P("dp", None, "gz", "gy", None), P("dp", None, "gz", "gy", None), P(), P())
    return jax.shard_map(
        per_device, mesh=mesh, in_specs=in_specs, out_specs=out_specs, check_vma=False
    )
```

```python
import functools

import jax
import jax.numpy as jnp
from jax import lax
from jax.experimental import pallas as pl
from jax.experimental.pallas import tpu as pltpu
from jax.sharding import PartitionSpec as P

LEAK = 0.3
REACH = 3
AXES = ("dp", "pipe", "gz", "gy")
F32 = jnp.float32
BF16 = jnp.bfloat16
PARAMS = pltpu.CompilerParams(vmem_limit_bytes=48 * 1024 * 1024)


def pairs(count, odd):
    out = []
    for i in range(odd, count - 1, 2):
        out += [(i, i + 1), (i + 1, i)]
    return out


def swap(cells, plan, kind):
    z_kind, y_kind = kind
    if plan.split:
        perm = []
        for d in range(plan.dp):
            for p in range(2):
                for a in range(plan.gz):
                    for c in range(plan.gy):
                        to = [d, p, a if z_kind is None else 1 - a, c]
                        if y_kind is not None:
                            near = c + 2 * p - 1
                            if 0 <= near < plan.gy:
                                to[1], to[3] = 1 - p, near
                            else:
                                to = [d ^ 1 if d ^ 1 < plan.dp else d, p, a, c]
                        perm.append((plan.index(d, p, a, c), plan.index(*to)))
        return lax.ppermute(cells, AXES, perm)
    z_list = [(i, i) for i in range(plan.gz)] if z_kind is None else pairs(plan.gz, z_kind)
    y_list = [(i, i) for i in range(plan.gy)] if y_kind is None else pairs(plan.gy, y_kind)
    perm = [(a * plan.gy + c, b * plan.gy + d) for a, b in z_list for c, d in y_list]
    return lax.ppermute(cells, ("gz", "gy"), perm)


def shift(block, step, width):
    parts = []
    for at in range(0, block.shape[1], width):
        part = block[:, at : at + width]
        lane = lax.broadcasted_iota(jnp.int32, part.shape, 1)
        edge = 0 if step > 0 else width - 1
        parts.append(jnp.where(lane == edge, 0.0, pltpu.roll(part, step % width, 1)))
    return parts[0] if len(parts) == 1 else jnp.concatenate(parts, axis=1)


class Plan:
    def __init__(self, volumes, cotangent, conv_one, conv_two):
        count, self.fold, self.z, self.y, self.x = volumes.shape
        self.c_one, self.c_in = conv_one.shape[:2]
        self.c_two = conv_two.shape[0]
        self.cz, self.cy = cotangent.shape[2:4]
        self.dp, self.pipe = lax.axis_size("dp"), lax.axis_size("pipe")
        self.gz, self.gy = lax.axis_size("gz"), lax.axis_size("gy")
        self.batch = count * self.dp
        self.split = count == self.gz == self.pipe == 2 and self.y % 4 == 0 and self.y >= 2 * REACH
        self.h = min(REACH, self.z)
        sides = min(self.gz - 1, 2)
        if self.split:
            self.r, self.o = self.y // 2, 2 * self.z
            self.win = self.planes = self.o
            self.cot_planes = 2 * self.cz + 2
            self.kinds = [(None, None), (0, 0), (None, 0), (0, None)]
        else:
            self.r, self.o = self.y, self.z
            self.win = self.z + sides * self.h
            self.planes = self.z + sides
            self.cot_planes = self.cz + 2
            z_kinds = [None] + [k for k in (0, 1) if len(pairs(self.gz, k)) > 0]
            y_kinds = [None] + [k for k in (0, 1) if len(pairs(self.gy, k)) > 0]
            self.kinds = [(a, b) for a in z_kinds for b in y_kinds]
        self.wide = self.r + 2 * REACH
        self.mid = self.r + 4
        self.slim = self.r + 2

    def index(self, d, p, a, c):
        return ((d * self.pipe + p) * self.gz + a) * self.gy + c

    def at_z(self):
        if self.split or self.gz == 1:
            return 0, 0
        if self.gz > 2:
            return self.h, self.h - 1
        me = lax.axis_index("gz")
        return me * self.h, me * (self.h - 1)

    def row0(self):
        return lax.axis_index("pipe") * self.r if self.split else 0

    def blocks(self, kind):
        z_kind, y_kind = kind
        nz, nc = (self.z, self.cz) if z_kind is None or self.split else (self.h, 1)
        if y_kind is not None:
            ny, nr = REACH, 1
        elif z_kind is not None and self.split:
            ny, nr = self.r + REACH, self.r // 2 + 1
        else:
            ny, nr = self.y, self.cy
        return nz, ny, nc, nr

    def rows(self, kind):
        nz, ny, nc, nr = self.blocks(kind)
        return nz * ny * self.fold + nc * nr * self.c_two // 2


def message_key(plan, kind):
    z_kind, y_kind = kind
    if not plan.split and z_kind is not None and plan.h == plan.z and plan.cz == 1:
        z_kind = None
    return z_kind, y_kind


def pack_kernel(plan, keys, vol_hbm, cot_hbm, *refs):
    out_refs, (vol_ref, cot_ref, cells, cots, sems) = refs[: len(keys)], refs[len(keys) :]
    me, my_z, my_y = lax.axis_index("pipe"), lax.axis_index("gz"), lax.axis_index("gy")
    first = [my_z, 1 - my_z] if plan.split else [me]
    loads = []
    for v, volume in enumerate(first):
        loads.append(pltpu.make_async_copy(vol_hbm.at[volume], vol_ref.at[v], sems.at[2 * v]))
        loads.append(pltpu.make_async_copy(cot_hbm.at[volume], cot_ref.at[v], sems.at[2 * v + 1]))
    for load in loads:
        load.start()
    half = plan.c_two // 2
    for v in range(len(first)):
        loads[2 * v].wait()
        for z in range(plan.z):
            block = jnp.swapaxes(vol_ref[v, :, z].astype(F32), 0, 1).astype(BF16)
            for y in range(plan.y):
                cells[v, z, y] = block[y]
        loads[2 * v + 1].wait()
        for z in range(plan.cz):
            block = jnp.swapaxes(cot_ref[v, :, z].astype(F32), 0, 1)
            for r in range(plan.cy):
                row = jnp.concatenate([block[r][:half], block[r][half:]], axis=1)
                cots[v, z, r] = row.astype(BF16)
    for key, out_ref in zip(keys, out_refs):
        nz, ny, nc, nr = plan.blocks(key)
        z0 = c0 = y0 = r0 = 0
        v = 1 if plan.split and key[0] is not None else 0
        y_low = None
        if plan.split:
            if key != (None, None):
                y_low = me == 0
        else:
            if key[0] is not None:
                z_low = my_z % 2 == 1 - key[0]
                z0 = jnp.where(z_low, 0, plan.z - nz)
                c0 = jnp.where(z_low, 0, plan.cz - nc)
            if key[1] is not None:
                y_low = my_y % 2 == 1 - key[1]
        if y_low is not None:
            y0 = jnp.where(y_low, 0, plan.y - ny)
            r0 = jnp.where(y_low, 0, plan.cy - nr)
        at = 0
        for i in range(nz):
            for j in range(ny):
                out_ref[at : at + plan.fold] = cells[v, z0 + i, y0 + j]
                at += plan.fold
        for i in range(nc):
            for j in range(nr):
                out_ref[at : at + half] = cots[v, c0 + i, r0 + j]
                at += half


def weight_kernel(plan, one_hbm, two_hbm, w1_ref, w2_ref, wb_ref, one_ref, two_ref, sems):
    loads = [
        pltpu.make_async_copy(one_hbm, one_ref, sems.at[0]),
        pltpu.make_async_copy(two_hbm, two_ref, sems.at[1]),
    ]
    for load in loads:
        load.start()
    for load in loads:
        load.wait()
    c_in, c_one, c_two = plan.c_in, plan.c_one, plan.c_two
    none = jnp.zeros((c_in, c_one), F32)
    pairs_x = {}
    for dz in range(3):
        for dy in range(3):
            tap = [one_ref[(dz * 3 + dy) * 3 + dx].astype(F32) * 0.5 for dx in range(3)]
            pairs_x[dz, dy, 0] = jnp.concatenate(
                [jnp.concatenate([tap[1], tap[0]], 1), jnp.concatenate([tap[2], tap[1]], 1)], 0
            )
            pairs_x[dz, dy, 1] = jnp.concatenate(
                [jnp.concatenate([none, tap[2]], 1), jnp.concatenate([tap[0], none], 1)], 0
            )
    blank = jnp.zeros((2 * c_in, 2 * c_one), F32)
    rows = []
    for fz in range(4):
        for s in range(2):
            for fy in (1, 2, 3, 0):
                rows.append(
                    jnp.concatenate(
                        [
                            pairs_x.get((fz - a, fy - b, s), blank)
                            for a in range(2)
                            for b in range(2)
                        ],
                        axis=1,
                    )
                )
    w1_ref[...] = jnp.concatenate(rows, axis=0).T.astype(BF16)
    for dx in range(3):
        taps = [two_ref[zy * 3 + dx] for zy in range(9)]
        wb_ref[dx * c_one : (dx + 1) * c_one] = jnp.concatenate(taps, axis=1)
        tall = jnp.concatenate([t.astype(F32) * 0.5 for t in taps], axis=0)
        w2_ref[dx * c_two : (dx + 1) * c_two] = tall.T.astype(BF16)


def around(ref, w, lane, size, step, sign):
    return jnp.concatenate(
        [
            ref[w + 1 + sign * dz, :, lane + sign * dy * step : lane + sign * dy * step + size]
            for dz in (-1, 0, 1)
            for dy in (-1, 0, 1)
        ],
        axis=0,
    )


def forward_kernel(plan, count, *refs):
    msgs = refs[:count]
    w1_ref, w2_ref, keep_ref, give_ref, fine, act, sg, tan = refs[count : count + 8]
    cells, cot, sgx, total = refs[count + 8 :]
    X, Y, Z, R = plan.x, plan.y, plan.z, plan.r
    fold, c_in, c_one, c_two = plan.fold, plan.c_in, plan.c_one, plan.c_two
    me, my_z, my_y = lax.axis_index("pipe"), lax.axis_index("gz"), lax.axis_index("gy")
    own, first_sg = plan.at_z()
    row0 = plan.row0()
    low_ok, high_ok = my_y > 0, my_y < plan.gy - 1
    if plan.split:
        low_ok, high_ok = low_ok | (me == 1), high_ok | (me == 0)

    pick = (
        lax.broadcasted_iota(jnp.int32, (X, 2 * X), 1) // 2
        == lax.broadcasted_iota(jnp.int32, (X, 2 * X), 0)
    )
    pick = jnp.where(pick, 0.125, 0.0).astype(BF16)
    if not plan.split:
        cot[...] = jnp.zeros_like(cot)
    for kind, msg in zip(plan.kinds, msgs):
        nz, ny, nc, nr = plan.blocks(kind)
        z_kind, y_kind = kind
        below, used = None, None
        if plan.split:
            half = my_z if z_kind is None else 1 - my_z
            z0, c0 = half * Z, half * plan.cz + 1
            if y_kind is not None:
                below = me == 0
                used = (below & (my_y > 0)) | ((me == 1) & (my_y < plan.gy - 1))
        else:
            z0, c0 = own, 1
            if z_kind is not None:
                before = my_z % 2 == 1 - z_kind
                z0 = jnp.clip(jnp.where(before, own - plan.h, own + Z), 0, plan.win - plan.h)
                c0 = jnp.where(before, 0, plan.cz + 1)
            if y_kind is not None:
                below = my_y % 2 == 1 - y_kind
        y0, r0 = REACH, 0
        if y_kind is not None:
            y0 = jnp.where(below, 0, Y + REACH)
        elif z_kind is not None and plan.split:
            y0, r0 = REACH + me * (Y - ny), me * (plan.cy - nr)
        at = 0
        for i in range(nz):
            for j in range(ny):
                block = msg[at : at + fold]
                if used is not None:
                    block = jnp.where(used, block, jnp.zeros_like(block))
                cells[z0 + i, y0 + j] = block
                at += fold
        part = c_two // 2
        up = jnp.dot(msg[at : at + nc * nr * part], pick, preferred_element_type=F32)
        if used is not None:
            up = jnp.where(used, up, 0.0)
        up = up.astype(BF16)
        for i in range(nc):
            for j in range(nr):
                row = up[(i * nr + j) * part : (i * nr + j + 1) * part]
                if y_kind is None:
                    lanes = [(2 * (r0 + j) + 2) * X, (2 * (r0 + j) + 3) * X]
                else:
                    lanes = [jnp.where(below, X, (Y + 2) * X)]
                for lane in lanes:
                    if not isinstance(lane, int):
                        lane = pl.multiple_of(lane, X)
                    cot[c0 + i, :part, pl.ds(lane, X)] = row[:, :X]
                    cot[c0 + i, part:, pl.ds(lane, X)] = row[:, X:]

    quarter = 2 * c_in
    fine[0 : 8 * quarter] = jnp.zeros((8 * quarter, plan.mid * X), BF16)
    last = 8 * quarter + plan.win * 16 * quarter
    fine[last : last + 8 * quarter] = jnp.zeros((8 * quarter, plan.mid * X), BF16)
    is_c = (lax.broadcasted_iota(jnp.int32, (fold, X), 0) // c_in) % 2 == 1

    def spread(w, carry):
        base = pl.multiple_of(8 * quarter + w * 16 * quarter, 8 * quarter)
        kept = []
        for r in range(plan.wide):
            mid = cells[w, row0 + r].astype(F32)
            side = jnp.where(is_c, shift(mid, 1, X), shift(mid, -1, X))
            kept.append((mid, side))
            if r < 2:
                continue
            lane = (r - 2) * X
            for a in range(2):
                for s in range(2):
                    lo, here, hi = kept[r - 2][s], kept[r - 1][s], kept[r][s]
                    at = a * 2 * quarter
                    near = here[at : at + 2 * quarter]
                    far = jnp.concatenate(
                        [hi[at : at + quarter], lo[at + quarter : at + 2 * quarter]], axis=0
                    )
                    row = base + (a * 8 + s * 4) * quarter
                    fine[pl.ds(row, 2 * quarter), lane : lane + X] = near.astype(BF16)
                    fine[pl.ds(row + 2 * quarter, 2 * quarter), lane : lane + X] = far.astype(BF16)
        return carry

    lax.fori_loop(0, plan.win, spread, 0, unroll=True)

    w1 = w1_ref[...]
    last_q = plan.mid // 2 - 1
    act[0] = jnp.zeros(act.shape[1:], BF16)
    act[plan.win + 1] = jnp.zeros(act.shape[1:], BF16)

    def first_section(w, carry):
        top = pl.multiple_of(w * 16 * quarter, 8 * quarter)
        z_abs = my_z * Z + w - own
        z_ok = None if plan.split else (z_abs >= 0) & (z_abs < plan.gz * Z)
        for q in range(plan.mid // 2):
            lane = 2 * q * X
            half = jnp.dot(
                w1, fine[pl.ds(top, 32 * quarter), lane : lane + 2 * X], preferred_element_type=F32
            )
            line, prod = None, None
            for g in range(8):
                v = half[g * c_one : (g + 1) * c_one]
                t = jnp.tanh(v)
                if 0 < q < last_q:
                    tan[w, g * c_one : (g + 1) * c_one, lane - 2 * X : lane] = t
                bent = jnp.maximum(v, LEAK * v)
                grown = 1.0 + jnp.abs(t)
                line = bent if line is None else line + bent
                prod = grown if prod is None else prod * grown
            mean = 0.25 * line - ((1.0 - LEAK) / 8.0) * jnp.log(prod)
            for ok in (z_ok, low_ok if q == 0 else None, high_ok if q == last_q else None):
                if ok is not None:
                    mean = jnp.where(ok, mean, 0.0)
            act[w + 1, :, lane : lane + 2 * X] = mean.astype(BF16)
        return carry

    lax.fori_loop(0, plan.win, first_section, 0, unroll=True)

    w2 = w2_ref[...]
    sg[0] = jnp.zeros(sg.shape[1:], BF16)
    sg[plan.planes + 1] = jnp.zeros(sg.shape[1:], BF16)

    def second_section(j, carry):
        w = first_sg + j
        c_at = (w - own + 2) // 2
        for q in range(plan.slim // 2):
            lane = 2 * q * X
            taps = jnp.dot(w2, around(act, w, lane + X, 2 * X, X, 1), preferred_element_type=F32)
            half = (
                taps[c_two : 2 * c_two]
                + shift(taps[:c_two], 1, X)
                + shift(taps[2 * c_two :], -1, X)
            )
            slope = (LEAK + 1.0) / 2 + ((1.0 - LEAK) / 2) * jnp.tanh(half)
            near = pl.multiple_of((row0 + 1) * X + lane, X)
            part = cot[c_at, :, pl.ds(near, 2 * X)].astype(F32)
            sg[j + 1, :, lane : lane + 2 * X] = (slope * part).astype(BF16)
        return carry

    lax.fori_loop(0, plan.planes, second_section, 0, unroll=True)

    grad_two = None
    for i in range(plan.o):
        w, j = own + i, own + i - first_sg
        for y in range(R):
            mid = sg[j + 1, :, (y + 1) * X : (y + 2) * X]
            wide = mid.astype(F32)
            at = slice(y * X, (y + 1) * X)
            sgx[0:c_two, at] = shift(wide, -1, X).astype(BF16)
            sgx[c_two : 2 * c_two, at] = mid
            sgx[2 * c_two : 3 * c_two, at] = shift(wide, 1, X).astype(BF16)
        term = lax.dot_general(
            around(act, w, 2 * X, R * X, X, 1),
            sgx[...],
            (((1,), (1,)), ((), ())),
            preferred_element_type=F32,
        )
        grad_two = term if grad_two is None else grad_two + term
    nine = 9 * c_one
    total[0:nine] = grad_two[:, : 2 * c_two]
    total[nine : nine + nine // 2] = jnp.concatenate(
        [grad_two[: nine // 2, 2 * c_two :], grad_two[nine // 2 :, 2 * c_two :]], axis=1
    )
    rest = total.shape[0] - nine - nine // 2
    if rest > 0:
        total[nine + nine // 2 :] = jnp.zeros((rest, total.shape[1]), F32)
    rows = total.shape[0] // 2
    keep_ref[...] = total[pl.ds(pl.multiple_of(me * rows, rows), rows)]
    give_ref[...] = total[pl.ds(pl.multiple_of((1 - me) * rows, rows), rows)].astype(BF16)


def backward_kernel(plan, wb_ref, fine, act, sg, tan, one_ref, *refs):
    out_refs, (back, first) = refs[:-2], refs[-2:]
    X, Z, R = plan.x, plan.z, plan.r
    c_in, c_one = plan.c_in, plan.c_one
    quarter = 2 * c_in
    own, first_sg = plan.at_z()
    wb = wb_ref[...]
    tall = []
    for i in range(plan.o):
        w, j = own + i, own + i - first_sg
        for q in range(R // 2):
            lane = 2 * q * X
            taps = jnp.dot(wb, around(sg, j, lane + X, 2 * X, X, -1), preferred_element_type=F32)
            grad = (
                taps[c_one : 2 * c_one]
                + shift(taps[:c_one], -1, X)
                + shift(taps[2 * c_one :], 1, X)
            ).astype(BF16)
            back[i, :, lane : lane + 2 * X] = grad
            grad = grad.astype(F32) * 0.125
            for g in range(8):
                t = tan[w, g * c_one : (g + 1) * c_one, lane : lane + 2 * X]
                slope = (LEAK + 1.0) / 2 + ((1.0 - LEAK) / 2) * t
                at = (i * R + 2 * q) * X
                first[g * c_one : (g + 1) * c_one, at : at + 2 * X] = (slope * grad).astype(BF16)
        top = w * 16 * quarter
        if not isinstance(top, int):
            top = pl.multiple_of(top, 8 * quarter)
        tall.append(fine[pl.ds(top, 32 * quarter), 2 * X : (2 + R) * X])
    grad_one = lax.dot_general(
        jnp.concatenate(tall, axis=1),
        first[...],
        (((1,), (1,)), ((), ())),
        preferred_element_type=F32,
    )
    half = 4 * c_one
    third = 8 * quarter
    folded = grad_one[: 3 * third, :half] + grad_one[third:, half:]
    place = {1: 0, 2: 1, 3: 2, 0: 3}

    def piece(dz, s, fy):
        row = dz * third + (s * 4 + place[fy]) * quarter
        return folded[row : row + quarter]

    taps = []
    up, down = slice(0, c_in), slice(c_in, 2 * c_in)
    left, right = slice(0, c_one), slice(c_one, 2 * c_one)
    for dz in range(3):
        for dy in range(3):
            mid, side = (
                piece(dz, s, dy)[:, : half // 2] + piece(dz, s, dy + 1)[:, half // 2 :]
                for s in range(2)
            )
            taps.append(side[down, left] + mid[up, right])
            taps.append(mid[up, left] + mid[down, right])
            taps.append(mid[down, left] + side[up, right])
    per = one_ref.shape[1] // c_one
    taps += [jnp.zeros((c_in, c_one), F32)] * (-len(taps) % (2 * per))
    for at in range(0, len(taps), 2 * per):
        pair = [jnp.concatenate(taps[at + k : at + k + per], axis=1) for k in (0, per)]
        row = at // per * c_in
        one_ref[row : row + 2 * c_in] = jnp.concatenate(pair, axis=0)
    done = len(taps) // per * c_in
    if done < one_ref.shape[0]:
        one_ref[done:] = jnp.zeros((one_ref.shape[0] - done, one_ref.shape[1]), F32)

    for k, out_ref in enumerate(out_refs):
        z0 = 0
        if plan.split:
            my_z = lax.axis_index("gz")
            z0 = (my_z if k == 0 else 1 - my_z) * Z
        for i in range(Z):
            for y in range(R):
                out_ref[0, i, y] = act[own + z0 + i + 1, :, (2 + y) * X : (3 + y) * X]
                out_ref[1, i, y] = back[z0 + i, :, y * X : (y + 1) * X]


def join_kernel(plan, *refs):
    parts, outs = refs[:-2], refs[-2:]
    me = lax.axis_index("pipe")
    my_z = lax.axis_index("gz")
    for i in range(plan.z):
        for kind, out_ref in enumerate(outs):
            if plan.split:
                mine, theirs, mine_far, theirs_far = parts
                for v, (here, far) in enumerate(((mine, mine_far), (theirs, theirs_far))):
                    one, two = here[kind, i].astype(F32), far[kind, i].astype(F32)
                    low, high = jnp.where(me == 0, one, two), jnp.where(me == 0, two, one)
                    lines = jnp.concatenate([low, high], axis=0)
                    at = my_z if v == 0 else 1 - my_z
                    out_ref[at, :, i] = jnp.swapaxes(lines, 0, 1).astype(BF16)
            else:
                for v, part in enumerate(parts):
                    at = me if v == 0 else 1 - me
                    lines = part[kind, i].astype(F32)
                    out_ref[at, :, i] = jnp.swapaxes(lines, 0, 1).astype(BF16)


def unpack_kernel(plan, own_ref, other_ref, one_ref, two_ref, full):
    c_in, c_one, c_two = plan.c_in, plan.c_one, plan.c_two
    me = lax.axis_index("pipe")
    rows = full.shape[0] // 2
    scale = 1.0 / plan.batch
    full[pl.ds(pl.multiple_of(me * rows, rows), rows)] = own_ref[:rows] * scale
    full[pl.ds(pl.multiple_of((1 - me) * rows, rows), rows)] = other_ref[:rows] * scale
    nine = 9 * c_one
    for zy in range(9):
        block = full[zy * c_one : (zy + 1) * c_one]
        two_ref[zy * 3] = block[:, :c_two]
        two_ref[zy * 3 + 1] = block[:, c_two:]
    part = c_one // 2
    for p in range(18):
        at = nine + (p % 9) * part
        lane = (p // 9) * c_two
        two_ref[(p // 2) * 3 + 2, (p % 2) * part : (p % 2 + 1) * part] = full[
            at : at + part, lane : lane + c_two
        ]
    ones = (own_ref[rows:] + other_ref[rows:]) * scale
    per = ones.shape[1] // c_one
    for t in range(27):
        row, lane = t // per * c_in, t % per * c_one
        one_ref[t] = ones[row : row + c_in, lane : lane + c_one]


def vmem(count):
    return [pl.BlockSpec(memory_space=pltpu.VMEM)] * count


def shape(dims, dtype):
    return jax.ShapeDtypeStruct(dims, dtype)


def bits(axis):
    return [(axis, 1 << k) for k in range((lax.axis_size(axis) - 1).bit_length())]


def partner(plan, part, moves, other_moves=None):
    perm = []
    for d in range(plan.dp):
        for p in range(plan.pipe):
            for a in range(plan.gz):
                for c in range(plan.gy):
                    to = {"dp": d, "pipe": p, "gz": a, "gy": c}
                    for axis, step in moves if p == 0 or other_moves is None else other_moves:
                        to[axis] ^= step
                    perm.append((plan.index(d, p, a, c), plan.index(*to.values())))
    return lax.ppermute(part, AXES, perm)


def sum_replicas(plan, part):
    moves = bits("dp") + bits("gz") + bits("gy")
    steps = [moves[i : i + 2] for i in range(0, len(moves), 2)]
    if any(len(step) == 1 for step in steps):
        orders = zip(steps, steps)
    else:
        orders = zip(steps[::-1], steps)
    for here, there in orders:
        sent = part.astype(BF16)
        got = [partner(plan, sent, here[:1], there[:1]).astype(F32)]
        if len(here) > 1:
            got.append(partner(plan, sent, here[1:], there[1:]).astype(F32))
            got.append(partner(plan, sent, here, there).astype(F32))
        part = sent.astype(F32) + got[0]
        if len(here) > 1:
            part = part + (got[1] + got[2])
    return part


def per_device(volumes, conv_one, conv_two, cotangent):
    plan = Plan(volumes, cotangent, conv_one, conv_two)
    X, Y, Z, R = plan.x, plan.y, plan.z, plan.r
    c_in, c_one, c_two = plan.c_in, plan.c_one, plan.c_two
    keys = sorted({message_key(plan, k) for k in plan.kinds}, key=str)
    count = 2 if plan.split else 1
    sent = pl.pallas_call(
        functools.partial(pack_kernel, plan, keys),
        out_shape=[shape((plan.rows(k), X), BF16) for k in keys],
        in_specs=[pl.BlockSpec(memory_space=pltpu.HBM)] * 2,
        out_specs=vmem(len(keys)),
        scratch_shapes=[
            pltpu.VMEM((count,) + volumes.shape[1:], BF16),
            pltpu.VMEM((count,) + cotangent.shape[1:], BF16),
            pltpu.VMEM((count, Z, Y, plan.fold, X), BF16),
            pltpu.VMEM((count, plan.cz, plan.cy, c_two // 2, X), BF16),
            pltpu.SemaphoreType.DMA((2 * count,)),
        ],
        compiler_params=PARAMS,
        name="pack",
    )(*[pltpu.with_memory_space_constraint(a, pltpu.HBM) for a in (volumes, cotangent)])
    sent = dict(zip(keys, sent))
    msgs = []
    for kind in plan.kinds:
        cells = sent[message_key(plan, kind)]
        msgs.append(cells if kind == (None, None) else swap(cells, plan, kind))

    w1, w2, wb = pl.pallas_call(
        functools.partial(weight_kernel, plan),
        out_shape=[
            shape((8 * c_one, 64 * c_in), BF16),
            shape((3 * c_two, 9 * c_one), BF16),
            shape((3 * c_one, 9 * c_two), BF16),
        ],
        in_specs=[pl.BlockSpec(memory_space=pltpu.HBM)] * 2,
        out_specs=vmem(3),
        scratch_shapes=[
            pltpu.VMEM((27, c_in, c_one), BF16),
            pltpu.VMEM((27, c_one, c_two), BF16),
            pltpu.SemaphoreType.DMA((2,)),
        ],
        compiler_params=PARAMS,
        cost_estimate=pl.CostEstimate(flops=10**7, bytes_accessed=10**6, transcendentals=0),
        name="weights",
    )(
        *[
            pltpu.with_memory_space_constraint(
                w.transpose(2, 3, 4, 1, 0).reshape(27, w.shape[1], w.shape[0]), pltpu.HBM
            )
            for w in (conv_one, conv_two)
        ]
    )

    wide = 2 * c_two
    two_rows = -(-27 * c_one // 64) * 16
    one_rows = -(-27 * c_in * c_one // (16 * wide)) * 16
    keep, give, fine, act, sg, tan = pl.pallas_call(
        functools.partial(forward_kernel, plan, len(msgs)),
        out_shape=[
            shape((two_rows, wide), F32),
            shape((two_rows, wide), BF16),
            shape(((plan.win + 1) * 32 * c_in, plan.mid * X), BF16),
            shape((plan.win + 2, c_one, plan.mid * X), BF16),
            shape((plan.planes + 2, c_two, plan.slim * X), BF16),
            shape((plan.win, 8 * c_one, R * X), F32),
        ],
        in_specs=vmem(len(msgs) + 2),
        out_specs=vmem(6),
        scratch_shapes=[
            pltpu.VMEM((plan.win, Y + 2 * REACH, plan.fold, X), BF16),
            pltpu.VMEM((plan.cot_planes, c_two, (Y + 4) * X), BF16),
            pltpu.VMEM((3 * c_two, R * X), BF16),
            pltpu.VMEM((2 * two_rows, wide), F32),
        ],
        compiler_params=PARAMS,
        name="forward",
    )(*msgs, w1, w2)

    both = [("pipe", 1)]
    part = keep + partner(plan, give, both).astype(F32)
    blocks = shape((2, Z, R, c_one, X), BF16)
    one, *outs = pl.pallas_call(
        functools.partial(backward_kernel, plan),
        out_shape=[shape((one_rows, wide), F32)] + [blocks] * (2 if plan.split else 1),
        in_specs=vmem(5),
        out_specs=vmem(3 if plan.split else 2),
        scratch_shapes=[
            pltpu.VMEM((plan.o, c_one, R * X), BF16),
            pltpu.VMEM((8 * c_one, plan.o * R * X), BF16),
        ],
        compiler_params=PARAMS,
        cost_estimate=pl.CostEstimate(flops=10**9, bytes_accessed=10**7, transcendentals=0),
        name="backward",
    )(wb, fine, act, sg, tan)

    part = sum_replicas(plan, jnp.concatenate([part, one], axis=0))
    rest = partner(plan, part, both)
    if plan.split:
        outs = [outs[0], partner(plan, outs[1], [("gz", 1)])]
    outs = outs + [partner(plan, out, both) for out in outs]
    size = (2, c_one, Z, Y, X)
    all_act, all_back = pl.pallas_call(
        functools.partial(join_kernel, plan),
        out_shape=[shape(size, BF16)] * 2,
        in_specs=vmem(len(outs)),
        out_specs=vmem(2),
        compiler_params=PARAMS,
        name="join",
    )(*outs)
    grad_one, grad_two = pl.pallas_call(
        functools.partial(unpack_kernel, plan),
        out_shape=[shape((27, c_in, c_one), F32), shape((27, c_one, c_two), F32)],
        in_specs=vmem(2),
        out_specs=vmem(2),
        scratch_shapes=[pltpu.VMEM((2 * two_rows, wide), F32)],
        compiler_params=PARAMS,
        name="unpack",
    )(part, rest)
    grad_one = grad_one.reshape(3, 3, 3, c_in, c_one).transpose(4, 3, 0, 1, 2)
    grad_two = grad_two.reshape(3, 3, 3, c_one, c_two).transpose(4, 3, 0, 1, 2)
    return all_act, all_back, grad_one, grad_two


def solution(mesh):
    in_specs = (P("dp", None, "gz", "gy", None), P(), P(), P("dp", None, "gz", "gy", None))
    out_specs = (P("dp", None, "gz", "gy", None), P("dp", None, "gz", "gy", None), P(), P())
    return jax.shard_map(
        per_device, mesh=mesh, in_specs=in_specs, out_specs=out_specs, check_vma=False
    )
```

```python
import functools

import jax
import jax.numpy as jnp
from jax import lax
from jax.experimental import pallas as pl
from jax.experimental.pallas import tpu as pltpu
from jax.sharding import PartitionSpec as P

LEAK = 0.3
STEP = 3
REACH = 3
AXES = ("dp", "pipe", "gz", "gy")
F32 = jnp.float32
BF16 = jnp.bfloat16
PARAMS = pltpu.CompilerParams(vmem_limit_bytes=48 * 1024 * 1024)


def pairs(count, odd):
    out = []
    for i in range(odd, count - 1, 2):
        out += [(i, i + 1), (i + 1, i)]
    return out


def swap(cells, plan, kind):
    z_kind, y_kind = kind
    if plan.split:
        perm = []
        for d in range(plan.dp):
            for p in range(2):
                for a in range(plan.gz):
                    for c in range(plan.gy):
                        to = [d, p, a if z_kind is None else 1 - a, c]
                        if y_kind is not None:
                            near = c + 2 * p - 1
                            if 0 <= near < plan.gy:
                                to[1], to[3] = 1 - p, near
                            else:
                                to = [d ^ 1 if d ^ 1 < plan.dp else d, p, a, c]
                        perm.append((plan.index(d, p, a, c), plan.index(*to)))
        return lax.ppermute(cells, AXES, perm)
    z_list = [(i, i) for i in range(plan.gz)] if z_kind is None else pairs(plan.gz, z_kind)
    y_list = [(i, i) for i in range(plan.gy)] if y_kind is None else pairs(plan.gy, y_kind)
    perm = [(a * plan.gy + c, b * plan.gy + d) for a, b in z_list for c, d in y_list]
    return lax.ppermute(cells, ("gz", "gy"), perm)


def aligned(at, step):
    return at if isinstance(at, int) else pl.multiple_of(at, step)


def shift(block, step, width):
    parts = []
    for at in range(0, block.shape[1], width):
        part = block[:, at : at + width]
        lane = lax.broadcasted_iota(jnp.int32, part.shape, 1)
        edge = 0 if step > 0 else width - 1
        parts.append(jnp.where(lane == edge, 0.0, pltpu.roll(part, step % width, 1)))
    return parts[0] if len(parts) == 1 else jnp.concatenate(parts, axis=1)


class Plan:
    def __init__(self, volumes, cotangent, conv_one, conv_two):
        count, self.fold, self.z, self.y, self.x = volumes.shape
        self.c_one, self.c_in = conv_one.shape[:2]
        self.c_two = conv_two.shape[0]
        self.cz, self.cy = cotangent.shape[2:4]
        self.dp, self.pipe = lax.axis_size("dp"), lax.axis_size("pipe")
        self.gz, self.gy = lax.axis_size("gz"), lax.axis_size("gy")
        self.batch = count * self.dp
        self.split = count == self.gz == self.pipe == 2 and self.y % 4 == 0 and self.y >= 2 * REACH
        self.h = min(REACH, self.z)
        sides = min(self.gz - 1, 2)
        if self.split:
            self.r, self.o = self.y // 2, 2 * self.z
            self.win = self.planes = self.o
            self.cot_planes = 2 * self.cz + 2
            self.kinds = [(None, None), (0, 0), (None, 0), (0, None)]
        else:
            self.r, self.o = self.y, self.z
            self.win = self.z + sides * self.h
            self.planes = self.z + sides
            self.cot_planes = self.cz + 2
            z_kinds = [None] + [k for k in (0, 1) if len(pairs(self.gz, k)) > 0]
            y_kinds = [None] + [k for k in (0, 1) if len(pairs(self.gy, k)) > 0]
            self.kinds = [(a, b) for a in z_kinds for b in y_kinds]
        self.wide = self.r + 2 * REACH
        self.mid = self.r + 4
        self.slim = self.r + 2

    def index(self, d, p, a, c):
        return ((d * self.pipe + p) * self.gz + a) * self.gy + c

    def at_z(self):
        if self.split or self.gz == 1:
            return 0, 0
        if self.gz > 2:
            return self.h, self.h - 1
        me = lax.axis_index("gz")
        return me * self.h, me * (self.h - 1)

    def row0(self):
        return lax.axis_index("pipe") * self.r if self.split else 0

    def blocks(self, kind):
        z_kind, y_kind = kind
        nz, nc = (self.z, self.cz) if z_kind is None or self.split else (self.h, 1)
        if y_kind is not None:
            ny, nr = REACH, 1
        elif z_kind is not None and self.split:
            ny, nr = self.r + REACH, self.r // 2 + 1
        else:
            ny, nr = self.y, self.cy
        return nz, ny, nc, nr

    def rows(self, kind):
        nz, ny, nc, nr = self.blocks(kind)
        return nz * ny * self.fold + nc * nr * self.c_two // 2


def message_key(plan, kind):
    z_kind, y_kind = kind
    if not plan.split and z_kind is not None and plan.h == plan.z and plan.cz == 1:
        z_kind = None
    return z_kind, y_kind


def pack_kernel(plan, keys, vol_hbm, cot_hbm, *refs):
    out_refs, (vol_ref, cot_ref, cells, cots, sems) = refs[: len(keys)], refs[len(keys) :]
    me, my_z, my_y = lax.axis_index("pipe"), lax.axis_index("gz"), lax.axis_index("gy")
    first = [my_z, 1 - my_z] if plan.split else [me]
    loads = []
    for v, volume in enumerate(first):
        loads.append(pltpu.make_async_copy(vol_hbm.at[volume], vol_ref.at[v], sems.at[2 * v]))
        loads.append(pltpu.make_async_copy(cot_hbm.at[volume], cot_ref.at[v], sems.at[2 * v + 1]))
    for load in loads[1::2] + loads[::2]:
        load.start()
    half = plan.c_two // 2
    for v in range(len(first)):
        loads[2 * v + 1].wait()
        for z in range(plan.cz):
            block = jnp.swapaxes(cot_ref[v, :, z].astype(F32), 0, 1)
            for r in range(plan.cy):
                row = jnp.concatenate([block[r][:half], block[r][half:]], axis=1)
                cots[v, z, r] = row.astype(BF16)
    for v in range(len(first)):
        loads[2 * v].wait()
        for z in range(plan.z):
            block = jnp.swapaxes(vol_ref[v, :, z].astype(F32), 0, 1).astype(BF16)
            for y in range(plan.y):
                cells[v, z, y] = block[y]
    for key, out_ref in zip(keys, out_refs):
        nz, ny, nc, nr = plan.blocks(key)
        z0 = c0 = y0 = r0 = 0
        v = 1 if plan.split and key[0] is not None else 0
        y_low = None
        if plan.split:
            if key != (None, None):
                y_low = me == 0
        else:
            if key[0] is not None:
                z_low = my_z % 2 == 1 - key[0]
                z0 = jnp.where(z_low, 0, plan.z - nz)
                c0 = jnp.where(z_low, 0, plan.cz - nc)
            if key[1] is not None:
                y_low = my_y % 2 == 1 - key[1]
        if y_low is not None:
            y0 = jnp.where(y_low, 0, plan.y - ny)
            r0 = jnp.where(y_low, 0, plan.cy - nr)
        at = 0
        for i in range(nz):
            for j in range(ny):
                out_ref[at : at + plan.fold] = cells[v, z0 + i, y0 + j]
                at += plan.fold
        for i in range(nc):
            for j in range(nr):
                out_ref[at : at + half] = cots[v, c0 + i, r0 + j]
                at += half


def weight_kernel(plan, one_hbm, two_hbm, w1_ref, w2_ref, wb_ref, one_ref, two_ref, sems):
    loads = [
        pltpu.make_async_copy(one_hbm, one_ref, sems.at[0]),
        pltpu.make_async_copy(two_hbm, two_ref, sems.at[1]),
    ]
    for load in loads:
        load.start()
    for load in loads:
        load.wait()
    c_in, c_one, c_two = plan.c_in, plan.c_one, plan.c_two
    none = jnp.zeros((c_in, c_one), F32)
    pairs_x = {}
    for dz in range(3):
        for dy in range(3):
            tap = [one_ref[(dz * 3 + dy) * 3 + dx].astype(F32) * 0.5 for dx in range(3)]
            pairs_x[dz, dy, 0] = jnp.concatenate(
                [jnp.concatenate([tap[1], tap[0]], 1), jnp.concatenate([tap[2], tap[1]], 1)], 0
            )
            pairs_x[dz, dy, 1] = jnp.concatenate(
                [jnp.concatenate([none, tap[2]], 1), jnp.concatenate([tap[0], none], 1)], 0
            )
    blank = jnp.zeros((2 * c_in, 2 * c_one), F32)
    rows = []
    for fz in range(4):
        for s in range(2):
            for fy in (1, 2, 3, 0):
                rows.append(
                    jnp.concatenate(
                        [
                            pairs_x.get((fz - a, fy - b, s), blank)
                            for a in range(2)
                            for b in range(2)
                        ],
                        axis=1,
                    )
                )
    w1_ref[...] = jnp.concatenate(rows, axis=0).T.astype(BF16)
    for dx in range(3):
        taps = [two_ref[zy * 3 + dx] for zy in range(9)]
        wb_ref[dx * c_one : (dx + 1) * c_one] = jnp.concatenate(taps, axis=1)
        tall = jnp.concatenate([t.astype(F32) * 0.5 for t in taps], axis=0)
        w2_ref[dx * c_two : (dx + 1) * c_two] = tall.T.astype(BF16)


def around(ref, w, lane, size, step, sign):
    return jnp.concatenate(
        [
            ref[w + 1 + sign * dz, :, lane + sign * dy * step : lane + sign * dy * step + size]
            for dz in (-1, 0, 1)
            for dy in (-1, 0, 1)
        ],
        axis=0,
    )


def each(plan, count, body):
    if plan.split:
        for i in range(count):
            body(i, 0)
    else:
        lax.fori_loop(0, count, body, 0)


def forward_kernel(plan, count, *refs):
    msgs = refs[:count]
    w1_ref, w2_ref, keep_ref, give_ref, fine, act, sg, tan = refs[count : count + 8]
    cells, cot, sgx, total = refs[count + 8 :]
    X, Y, Z, R = plan.x, plan.y, plan.z, plan.r
    fold, c_in, c_one, c_two = plan.fold, plan.c_in, plan.c_one, plan.c_two
    me, my_z, my_y = lax.axis_index("pipe"), lax.axis_index("gz"), lax.axis_index("gy")
    own, first_sg = plan.at_z()
    row0 = plan.row0()
    low_ok, high_ok = my_y > 0, my_y < plan.gy - 1
    if plan.split:
        low_ok, high_ok = low_ok | (me == 1), high_ok | (me == 0)

    pick = (
        lax.broadcasted_iota(jnp.int32, (X, 2 * X), 1) // 2
        == lax.broadcasted_iota(jnp.int32, (X, 2 * X), 0)
    )
    pick = jnp.where(pick, 0.125, 0.0).astype(BF16)
    if not plan.split:
        cot[...] = jnp.zeros_like(cot)
    for kind, msg in zip(plan.kinds, msgs):
        nz, ny, nc, nr = plan.blocks(kind)
        z_kind, y_kind = kind
        below, used = None, None
        if plan.split:
            half = my_z if z_kind is None else 1 - my_z
            z0, c0 = half * Z, half * plan.cz + 1
            if y_kind is not None:
                below = me == 0
                used = (below & (my_y > 0)) | ((me == 1) & (my_y < plan.gy - 1))
        else:
            z0, c0 = own, 1
            if z_kind is not None:
                before = my_z % 2 == 1 - z_kind
                z0 = jnp.clip(jnp.where(before, own - plan.h, own + Z), 0, plan.win - plan.h)
                c0 = jnp.where(before, 0, plan.cz + 1)
            if y_kind is not None:
                below = my_y % 2 == 1 - y_kind
        y0, r0 = REACH, 0
        if y_kind is not None:
            y0 = jnp.where(below, 0, Y + REACH)
        elif z_kind is not None and plan.split:
            y0, r0 = REACH + me * (Y - ny), me * (plan.cy - nr)
        at = 0
        for i in range(nz):
            for j in range(ny):
                block = msg[at : at + fold]
                if used is not None:
                    block = jnp.where(used, block, jnp.zeros_like(block))
                cells[z0 + i, y0 + j] = block
                at += fold
        part = c_two // 2
        up = jnp.dot(msg[at : at + nc * nr * part], pick, preferred_element_type=F32)
        if used is not None:
            up = jnp.where(used, up, 0.0)
        up = up.astype(BF16)
        for i in range(nc):
            for j in range(nr):
                row = up[(i * nr + j) * part : (i * nr + j + 1) * part]
                if y_kind is None:
                    lanes = [(2 * (r0 + j) + 2) * X, (2 * (r0 + j) + 3) * X]
                else:
                    lanes = [jnp.where(below, X, (Y + 2) * X)]
                for lane in lanes:
                    lane = aligned(lane, X)
                    cot[c0 + i, :part, pl.ds(lane, X)] = row[:, :X]
                    cot[c0 + i, part:, pl.ds(lane, X)] = row[:, X:]

    quarter = 2 * c_in
    fine[0 : 8 * quarter] = jnp.zeros((8 * quarter, plan.mid * X), BF16)
    last = 8 * quarter + plan.win * 16 * quarter
    fine[last : last + 8 * quarter] = jnp.zeros((8 * quarter, plan.mid * X), BF16)
    is_c = (lax.broadcasted_iota(jnp.int32, (fold, X), 0) // c_in) % 2 == 1

    def spread(w, carry):
        base = aligned(8 * quarter + w * 16 * quarter, 8 * quarter)
        kept = []
        for r in range(plan.wide):
            mid = cells[w, row0 + r].astype(F32)
            side = jnp.where(is_c, shift(mid, 1, X), shift(mid, -1, X))
            kept.append((mid, side))
            if r < 2:
                continue
            lane = (r - 2) * X
            for a in range(2):
                for s in range(2):
                    lo, here, hi = kept[r - 2][s], kept[r - 1][s], kept[r][s]
                    at = a * 2 * quarter
                    near = here[at : at + 2 * quarter]
                    far = jnp.concatenate(
                        [hi[at : at + quarter], lo[at + quarter : at + 2 * quarter]], axis=0
                    )
                    row = base + (a * 8 + s * 4) * quarter
                    fine[pl.ds(row, 2 * quarter), lane : lane + X] = near.astype(BF16)
                    fine[pl.ds(row + 2 * quarter, 2 * quarter), lane : lane + X] = far.astype(BF16)
        return carry

    each(plan, plan.win, spread)

    w1 = w1_ref[...]
    last_q = plan.mid // 2 - 1
    act[0] = jnp.zeros(act.shape[1:], BF16)
    act[plan.win + 1] = jnp.zeros(act.shape[1:], BF16)

    def first_section(w, carry):
        top = aligned(w * 16 * quarter, 8 * quarter)
        z_abs = my_z * Z + w - own
        z_ok = None if plan.split else (z_abs >= 0) & (z_abs < plan.gz * Z)
        for q in range(plan.mid // 2):
            lane = 2 * q * X
            half = jnp.dot(
                w1, fine[pl.ds(top, 32 * quarter), lane : lane + 2 * X], preferred_element_type=F32
            )
            line, prod = None, None
            for g in range(8):
                v = half[g * c_one : (g + 1) * c_one]
                t = jnp.tanh(v)
                if 0 < q < last_q:
                    tan[w, g * c_one : (g + 1) * c_one, lane - 2 * X : lane] = t
                bent = jnp.maximum(v, LEAK * v)
                grown = 1.0 + jnp.abs(t)
                line = bent if line is None else line + bent
                prod = grown if prod is None else prod * grown
            mean = 0.25 * line - ((1.0 - LEAK) / 8.0) * jnp.log(prod)
            for ok in (z_ok, low_ok if q == 0 else None, high_ok if q == last_q else None):
                if ok is not None:
                    mean = jnp.where(ok, mean, 0.0)
            act[w + 1, :, lane : lane + 2 * X] = mean.astype(BF16)
        return carry

    each(plan, plan.win, first_section)

    w2 = w2_ref[...]
    sg[0] = jnp.zeros(sg.shape[1:], BF16)
    sg[plan.planes + 1] = jnp.zeros(sg.shape[1:], BF16)

    def second_section(j, carry):
        w = first_sg + j
        c_at = (w - own + 2) // 2
        for q in range(plan.slim // 2):
            lane = 2 * q * X
            taps = jnp.dot(w2, around(act, w, lane + X, 2 * X, X, 1), preferred_element_type=F32)
            half = (
                taps[c_two : 2 * c_two]
                + shift(taps[:c_two], 1, X)
                + shift(taps[2 * c_two :], -1, X)
            )
            slope = (LEAK + 1.0) / 2 + ((1.0 - LEAK) / 2) * jnp.tanh(half)
            near = pl.multiple_of((row0 + 1) * X + lane, X)
            part = cot[c_at, :, pl.ds(near, 2 * X)].astype(F32)
            sg[j + 1, :, lane : lane + 2 * X] = (slope * part).astype(BF16)
        return carry

    each(plan, plan.planes, second_section)

    grad_two = None
    for i in range(plan.o):
        w, j = own + i, own + i - first_sg
        for y in range(R):
            mid = sg[j + 1, :, (y + 1) * X : (y + 2) * X]
            wide = mid.astype(F32)
            at = slice(y * X, (y + 1) * X)
            sgx[0:c_two, at] = shift(wide, -1, X).astype(BF16)
            sgx[c_two : 2 * c_two, at] = mid
            sgx[2 * c_two : 3 * c_two, at] = shift(wide, 1, X).astype(BF16)
        term = lax.dot_general(
            around(act, w, 2 * X, R * X, X, 1),
            sgx[...],
            (((1,), (1,)), ((), ())),
            preferred_element_type=F32,
        )
        grad_two = term if grad_two is None else grad_two + term
    nine = 9 * c_one
    total[0:nine] = grad_two[:, : 2 * c_two]
    total[nine : nine + nine // 2] = jnp.concatenate(
        [grad_two[: nine // 2, 2 * c_two :], grad_two[nine // 2 :, 2 * c_two :]], axis=1
    )
    rest = total.shape[0] - nine - nine // 2
    if rest > 0:
        total[nine + nine // 2 :] = jnp.zeros((rest, total.shape[1]), F32)
    rows = total.shape[0] // 2
    keep_ref[...] = total[pl.ds(pl.multiple_of(me * rows, rows), rows)]
    give_ref[...] = total[pl.ds(pl.multiple_of((1 - me) * rows, rows), rows)].astype(BF16)


def backward_kernel(plan, wb_ref, fine, act, sg, tan, one_ref, *refs):
    out_refs, (back, first) = refs[:-2], refs[-2:]
    X, Z, R = plan.x, plan.z, plan.r
    c_in, c_one = plan.c_in, plan.c_one
    quarter = 2 * c_in
    own, first_sg = plan.at_z()
    wb = wb_ref[...]
    tall = []
    for i in range(plan.o):
        w, j = own + i, own + i - first_sg
        for q in range(R // 2):
            lane = 2 * q * X
            taps = jnp.dot(wb, around(sg, j, lane + X, 2 * X, X, -1), preferred_element_type=F32)
            grad = (
                taps[c_one : 2 * c_one]
                + shift(taps[:c_one], -1, X)
                + shift(taps[2 * c_one :], 1, X)
            ).astype(BF16)
            back[i, :, lane : lane + 2 * X] = grad
            grad = grad.astype(F32) * 0.125
            for g in range(8):
                t = tan[w, g * c_one : (g + 1) * c_one, lane : lane + 2 * X]
                slope = (LEAK + 1.0) / 2 + ((1.0 - LEAK) / 2) * t
                at = (i * R + 2 * q) * X
                first[g * c_one : (g + 1) * c_one, at : at + 2 * X] = (slope * grad).astype(BF16)
        top = aligned(w * 16 * quarter, 8 * quarter)
        tall.append(fine[pl.ds(top, 32 * quarter), 2 * X : (2 + R) * X])
    grad_one = lax.dot_general(
        jnp.concatenate(tall, axis=1),
        first[...],
        (((1,), (1,)), ((), ())),
        preferred_element_type=F32,
    )
    half = 4 * c_one
    third = 8 * quarter
    folded = grad_one[: 3 * third, :half] + grad_one[third:, half:]
    place = {1: 0, 2: 1, 3: 2, 0: 3}

    def piece(dz, s, fy):
        row = dz * third + (s * 4 + place[fy]) * quarter
        return folded[row : row + quarter]

    taps = []
    up, down = slice(0, c_in), slice(c_in, 2 * c_in)
    left, right = slice(0, c_one), slice(c_one, 2 * c_one)
    for dz in range(3):
        for dy in range(3):
            mid, side = (
                piece(dz, s, dy)[:, : half // 2] + piece(dz, s, dy + 1)[:, half // 2 :]
                for s in range(2)
            )
            taps.append(side[down, left] + mid[up, right])
            taps.append(mid[up, left] + mid[down, right])
            taps.append(mid[down, left] + side[up, right])
    per = one_ref.shape[1] // c_one
    taps += [jnp.zeros((c_in, c_one), F32)] * (-len(taps) % (2 * per))
    for at in range(0, len(taps), 2 * per):
        pair = [jnp.concatenate(taps[at + k : at + k + per], axis=1) for k in (0, per)]
        row = at // per * c_in
        one_ref[row : row + 2 * c_in] = jnp.concatenate(pair, axis=0)
    done = len(taps) // per * c_in
    if done < one_ref.shape[0]:
        one_ref[done:] = jnp.zeros((one_ref.shape[0] - done, one_ref.shape[1]), F32)

    for k, out_ref in enumerate(out_refs):
        z0 = 0
        if plan.split:
            my_z = lax.axis_index("gz")
            z0 = (my_z if k == 0 else 1 - my_z) * Z
        for i in range(Z):
            for y in range(R):
                out_ref[0, i, y] = act[own + z0 + i + 1, :, (2 + y) * X : (3 + y) * X]
                out_ref[1, i, y] = back[z0 + i, :, y * X : (y + 1) * X]


def join_kernel(plan, *refs):
    parts, outs = refs[:-2], refs[-2:]
    me = lax.axis_index("pipe")
    my_z = lax.axis_index("gz")
    for i in range(plan.z):
        for kind, out_ref in enumerate(outs):
            if plan.split:
                mine, theirs, mine_far, theirs_far = parts
                for v, (here, far) in enumerate(((mine, mine_far), (theirs, theirs_far))):
                    one, two = here[kind, i].astype(F32), far[kind, i].astype(F32)
                    low, high = jnp.where(me == 0, one, two), jnp.where(me == 0, two, one)
                    lines = jnp.concatenate([low, high], axis=0)
                    at = my_z if v == 0 else 1 - my_z
                    out_ref[at, :, i] = jnp.swapaxes(lines, 0, 1).astype(BF16)
            else:
                for v, part in enumerate(parts):
                    at = me if v == 0 else 1 - me
                    lines = part[kind, i].astype(F32)
                    out_ref[at, :, i] = jnp.swapaxes(lines, 0, 1).astype(BF16)


def unpack_kernel(plan, own_ref, other_ref, one_hbm, two_hbm, one_ref, two_ref, full, sems):
    c_in, c_one, c_two = plan.c_in, plan.c_one, plan.c_two
    me = lax.axis_index("pipe")
    rows = full.shape[0] // 2
    scale = 1.0 / plan.batch
    full[pl.ds(pl.multiple_of(me * rows, rows), rows)] = own_ref[:rows] * scale
    full[pl.ds(pl.multiple_of((1 - me) * rows, rows), rows)] = other_ref[:rows] * scale
    nine = 9 * c_one
    part = c_one // 2
    stores = []
    for zy in range(9):
        block = full[zy * c_one : (zy + 1) * c_one]
        two_ref[zy * 3] = block[:, :c_two]
        two_ref[zy * 3 + 1] = block[:, c_two:]
        for p in (2 * zy, 2 * zy + 1):
            at = nine + (p % 9) * part
            lane = (p // 9) * c_two
            two_ref[zy * 3 + 2, (p % 2) * part : (p % 2 + 1) * part] = full[
                at : at + part, lane : lane + c_two
            ]
        if zy % STEP == STEP - 1:
            at = pl.ds((zy - STEP + 1) * 3, 3 * STEP)
            stores.append(pltpu.make_async_copy(two_ref.at[at], two_hbm.at[at], sems.at[len(stores)]))
            stores[-1].start()
    ones = (own_ref[rows:] + other_ref[rows:]) * scale
    per = ones.shape[1] // c_one
    for t in range(27):
        row, lane = t // per * c_in, t % per * c_one
        one_ref[t] = ones[row : row + c_in, lane : lane + c_one]
    stores.append(pltpu.make_async_copy(one_ref, one_hbm, sems.at[len(stores)]))
    stores[-1].start()
    for store in stores:
        store.wait()


def vmem(count):
    return [pl.BlockSpec(memory_space=pltpu.VMEM)] * count


def shape(dims, dtype):
    return jax.ShapeDtypeStruct(dims, dtype)


def bits(axis):
    return [(axis, 1 << k) for k in range((lax.axis_size(axis) - 1).bit_length())]


def partner(plan, part, moves, other_moves=None):
    perm = []
    for d in range(plan.dp):
        for p in range(plan.pipe):
            for a in range(plan.gz):
                for c in range(plan.gy):
                    to = {"dp": d, "pipe": p, "gz": a, "gy": c}
                    for axis, step in moves if p == 0 or other_moves is None else other_moves:
                        to[axis] ^= step
                    perm.append((plan.index(d, p, a, c), plan.index(*to.values())))
    return lax.ppermute(part, AXES, perm)


def sum_replicas(plan, part):
    moves = bits("dp") + bits("gz") + bits("gy")
    steps = [moves[i : i + 2] for i in range(0, len(moves), 2)]
    if any(len(step) == 1 for step in steps):
        orders = zip(steps, steps)
    else:
        orders = zip(steps[::-1], steps)
    for here, there in orders:
        sent = part.astype(BF16)
        got = [partner(plan, sent, here[:1], there[:1]).astype(F32)]
        if len(here) > 1:
            got.append(partner(plan, sent, here[1:], there[1:]).astype(F32))
            got.append(partner(plan, sent, here, there).astype(F32))
        part = sent.astype(F32) + got[0]
        if len(here) > 1:
            part = part + (got[1] + got[2])
    return part


def per_device(volumes, conv_one, conv_two, cotangent):
    plan = Plan(volumes, cotangent, conv_one, conv_two)
    X, Y, Z, R = plan.x, plan.y, plan.z, plan.r
    c_in, c_one, c_two = plan.c_in, plan.c_one, plan.c_two
    keys = sorted({message_key(plan, k) for k in plan.kinds}, key=str)
    count = 2 if plan.split else 1
    sent = pl.pallas_call(
        functools.partial(pack_kernel, plan, keys),
        out_shape=[shape((plan.rows(k), X), BF16) for k in keys],
        in_specs=[pl.BlockSpec(memory_space=pltpu.HBM)] * 2,
        out_specs=vmem(len(keys)),
        scratch_shapes=[
            pltpu.VMEM((count,) + volumes.shape[1:], BF16),
            pltpu.VMEM((count,) + cotangent.shape[1:], BF16),
            pltpu.VMEM((count, Z, Y, plan.fold, X), BF16),
            pltpu.VMEM((count, plan.cz, plan.cy, c_two // 2, X), BF16),
            pltpu.SemaphoreType.DMA((2 * count,)),
        ],
        compiler_params=PARAMS,
        name="pack",
    )(*[pltpu.with_memory_space_constraint(a, pltpu.HBM) for a in (volumes, cotangent)])
    sent = dict(zip(keys, sent))
    msgs = []
    for kind in plan.kinds:
        cells = sent[message_key(plan, kind)]
        msgs.append(cells if kind == (None, None) else swap(cells, plan, kind))

    w1, w2, wb = pl.pallas_call(
        functools.partial(weight_kernel, plan),
        out_shape=[
            shape((8 * c_one, 64 * c_in), BF16),
            shape((3 * c_two, 9 * c_one), BF16),
            shape((3 * c_one, 9 * c_two), BF16),
        ],
        in_specs=[pl.BlockSpec(memory_space=pltpu.HBM)] * 2,
        out_specs=vmem(3),
        scratch_shapes=[
            pltpu.VMEM((27, c_in, c_one), BF16),
            pltpu.VMEM((27, c_one, c_two), BF16),
            pltpu.SemaphoreType.DMA((2,)),
        ],
        compiler_params=PARAMS,
        cost_estimate=pl.CostEstimate(flops=10**7, bytes_accessed=10**6, transcendentals=0),
        name="weights",
    )(
        *[
            pltpu.with_memory_space_constraint(
                w.transpose(2, 3, 4, 1, 0).reshape(27, w.shape[1], w.shape[0]), pltpu.HBM
            )
            for w in (conv_one, conv_two)
        ]
    )

    wide = 2 * c_two
    two_rows = -(-27 * c_one // 64) * 16
    one_rows = -(-27 * c_in * c_one // (16 * wide)) * 16
    keep, give, fine, act, sg, tan = pl.pallas_call(
        functools.partial(forward_kernel, plan, len(msgs)),
        out_shape=[
            shape((two_rows, wide), F32),
            shape((two_rows, wide), BF16),
            shape(((plan.win + 1) * 32 * c_in, plan.mid * X), BF16),
            shape((plan.win + 2, c_one, plan.mid * X), BF16),
            shape((plan.planes + 2, c_two, plan.slim * X), BF16),
            shape((plan.win, 8 * c_one, R * X), F32),
        ],
        in_specs=vmem(len(msgs) + 2),
        out_specs=vmem(6),
        scratch_shapes=[
            pltpu.VMEM((plan.win, Y + 2 * REACH, plan.fold, X), BF16),
            pltpu.VMEM((plan.cot_planes, c_two, (Y + 4) * X), BF16),
            pltpu.VMEM((3 * c_two, R * X), BF16),
            pltpu.VMEM((2 * two_rows, wide), F32),
        ],
        compiler_params=PARAMS,
        name="forward",
    )(*msgs, w1, w2)

    both = [("pipe", 1)]
    part = keep + partner(plan, give, both).astype(F32)
    blocks = shape((2, Z, R, c_one, X), BF16)
    one, *outs = pl.pallas_call(
        functools.partial(backward_kernel, plan),
        out_shape=[shape((one_rows, wide), F32)] + [blocks] * (2 if plan.split else 1),
        in_specs=vmem(5),
        out_specs=vmem(3 if plan.split else 2),
        scratch_shapes=[
            pltpu.VMEM((plan.o, c_one, R * X), BF16),
            pltpu.VMEM((8 * c_one, plan.o * R * X), BF16),
        ],
        compiler_params=PARAMS,
        cost_estimate=pl.CostEstimate(flops=10**9, bytes_accessed=10**7, transcendentals=0),
        name="backward",
    )(wb, fine, act, sg, tan)

    part = sum_replicas(plan, jnp.concatenate([part, one], axis=0))
    rest = partner(plan, part, both)
    if plan.split:
        outs = [outs[0], partner(plan, outs[1], [("gz", 1)])]
    outs = outs + [partner(plan, out, both) for out in outs]
    size = (2, c_one, Z, Y, X)
    all_act, all_back = pl.pallas_call(
        functools.partial(join_kernel, plan),
        out_shape=[shape(size, BF16)] * 2,
        in_specs=vmem(len(outs)),
        out_specs=vmem(2),
        compiler_params=PARAMS,
        name="join",
    )(*outs)
    grad_one, grad_two = pl.pallas_call(
        functools.partial(unpack_kernel, plan),
        out_shape=[shape((27, c_in, c_one), F32), shape((27, c_one, c_two), F32)],
        in_specs=vmem(2),
        out_specs=[pl.BlockSpec(memory_space=pltpu.HBM)] * 2,
        scratch_shapes=[
            pltpu.VMEM((27, c_in, c_one), F32),
            pltpu.VMEM((27, c_one, c_two), F32),
            pltpu.VMEM((2 * two_rows, wide), F32),
            pltpu.SemaphoreType.DMA((9 // STEP + 1,)),
        ],
        compiler_params=PARAMS,
        name="unpack",
    )(part, rest)
    grad_one = grad_one.reshape(3, 3, 3, c_in, c_one).transpose(4, 3, 0, 1, 2)
    grad_two = grad_two.reshape(3, 3, 3, c_one, c_two).transpose(4, 3, 0, 1, 2)
    return all_act, all_back, grad_one, grad_two


def solution(mesh):
    in_specs = (P("dp", None, "gz", "gy", None), P(), P(), P("dp", None, "gz", "gy", None))
    out_specs = (P("dp", None, "gz", "gy", None), P("dp", None, "gz", "gy", None), P(), P())
    return jax.shard_map(
        per_device, mesh=mesh, in_specs=in_specs, out_specs=out_specs, check_vma=False
    )
```

```python
import functools

import jax
import jax.numpy as jnp
from jax import lax
from jax.experimental import pallas as pl
from jax.experimental.pallas import tpu as pltpu
from jax.sharding import PartitionSpec as P

LEAK = 0.3
STEP = 3
REACH = 3
AXES = ("dp", "pipe", "gz", "gy")
F32 = jnp.float32
BF16 = jnp.bfloat16
PARAMS = pltpu.CompilerParams(vmem_limit_bytes=48 * 1024 * 1024)


def pairs(count, odd):
    out = []
    for i in range(odd, count - 1, 2):
        out += [(i, i + 1), (i + 1, i)]
    return out


def swap(cells, plan, kind):
    z_kind, y_kind = kind
    if plan.split:
        perm = []
        for d in range(plan.dp):
            for p in range(2):
                for a in range(plan.gz):
                    for c in range(plan.gy):
                        to = [d, p, a if z_kind is None else 1 - a, c]
                        if y_kind is not None:
                            near = c + 2 * p - 1
                            if 0 <= near < plan.gy:
                                to[1], to[3] = 1 - p, near
                            else:
                                to = [d ^ 1 if d ^ 1 < plan.dp else d, p, a, c]
                        perm.append((plan.index(d, p, a, c), plan.index(*to)))
        return lax.ppermute(cells, AXES, perm)
    z_list = [(i, i) for i in range(plan.gz)] if z_kind is None else pairs(plan.gz, z_kind)
    y_list = [(i, i) for i in range(plan.gy)] if y_kind is None else pairs(plan.gy, y_kind)
    perm = [(a * plan.gy + c, b * plan.gy + d) for a, b in z_list for c, d in y_list]
    return lax.ppermute(cells, ("gz", "gy"), perm)


def aligned(at, step):
    return at if isinstance(at, int) else pl.multiple_of(at, step)


def shift(block, step, width):
    parts = []
    for at in range(0, block.shape[1], width):
        part = block[:, at : at + width]
        lane = lax.broadcasted_iota(jnp.int32, part.shape, 1)
        edge = 0 if step > 0 else width - 1
        parts.append(jnp.where(lane == edge, 0.0, pltpu.roll(part, step % width, 1)))
    return parts[0] if len(parts) == 1 else jnp.concatenate(parts, axis=1)


class Plan:
    def __init__(self, volumes, cotangent, conv_one, conv_two):
        count, self.fold, self.z, self.y, self.x = volumes.shape
        self.c_one, self.c_in = conv_one.shape[:2]
        self.c_two = conv_two.shape[0]
        self.cz, self.cy = cotangent.shape[2:4]
        self.dp, self.pipe = lax.axis_size("dp"), lax.axis_size("pipe")
        self.gz, self.gy = lax.axis_size("gz"), lax.axis_size("gy")
        self.batch = count * self.dp
        self.split = count == self.gz == self.pipe == 2 and self.y % 4 == 0 and self.y >= 2 * REACH
        self.h = min(REACH, self.z)
        sides = min(self.gz - 1, 2)
        if self.split:
            self.r, self.o = self.y // 2, 2 * self.z
            self.win = self.planes = self.o
            self.cot_planes = 2 * self.cz + 2
            self.kinds = [(None, None), (0, 0), (None, 0), (0, None)]
        else:
            self.r, self.o = self.y, self.z
            self.win = self.z + sides * self.h
            self.planes = self.z + sides
            self.cot_planes = self.cz + 2
            z_kinds = [None] + [k for k in (0, 1) if len(pairs(self.gz, k)) > 0]
            y_kinds = [None] + [k for k in (0, 1) if len(pairs(self.gy, k)) > 0]
            self.kinds = [(a, b) for a in z_kinds for b in y_kinds]
        self.wide = self.r + 2 * REACH
        self.mid = self.r + 4
        self.slim = self.r + 2

    def index(self, d, p, a, c):
        return ((d * self.pipe + p) * self.gz + a) * self.gy + c

    def at_z(self):
        if self.split or self.gz == 1:
            return 0, 0
        if self.gz > 2:
            return self.h, self.h - 1
        me = lax.axis_index("gz")
        return me * self.h, me * (self.h - 1)

    def row0(self):
        return lax.axis_index("pipe") * self.r if self.split else 0

    def blocks(self, kind):
        z_kind, y_kind = kind
        nz, nc = (self.z, self.cz) if z_kind is None or self.split else (self.h, 1)
        if y_kind is not None:
            ny, nr = REACH, 1
        elif z_kind is not None and self.split:
            ny, nr = self.r + REACH, self.r // 2 + 1
        else:
            ny, nr = self.y, self.cy
        return nz, ny, nc, nr

    def rows(self, kind):
        nz, ny, nc, nr = self.blocks(kind)
        return nz * ny * self.fold + nc * nr * self.c_two // 2


def message_key(plan, kind):
    z_kind, y_kind = kind
    if not plan.split and z_kind is not None and plan.h == plan.z and plan.cz == 1:
        z_kind = None
    return z_kind, y_kind


def pack_kernel(plan, keys, vol_hbm, cot_hbm, *refs):
    out_refs, (vol_ref, cot_ref, cells, cots, sems) = refs[: len(keys)], refs[len(keys) :]
    me, my_z, my_y = lax.axis_index("pipe"), lax.axis_index("gz"), lax.axis_index("gy")
    first = [my_z, 1 - my_z] if plan.split else [me]
    loads = []
    for v, volume in enumerate(first):
        loads.append(pltpu.make_async_copy(vol_hbm.at[volume], vol_ref.at[v], sems.at[2 * v]))
        loads.append(pltpu.make_async_copy(cot_hbm.at[volume], cot_ref.at[v], sems.at[2 * v + 1]))
    for load in loads[1::2] + loads[::2]:
        load.start()
    half = plan.c_two // 2
    for v in range(len(first)):
        loads[2 * v + 1].wait()
        for z in range(plan.cz):
            block = jnp.swapaxes(cot_ref[v, :, z].astype(F32), 0, 1)
            for r in range(plan.cy):
                row = jnp.concatenate([block[r][:half], block[r][half:]], axis=1)
                cots[v, z, r] = row.astype(BF16)
    for v in range(len(first)):
        loads[2 * v].wait()
        for z in range(plan.z):
            block = jnp.swapaxes(vol_ref[v, :, z].astype(F32), 0, 1).astype(BF16)
            for y in range(plan.y):
                cells[v, z, y] = block[y]
    for key, out_ref in zip(keys, out_refs):
        nz, ny, nc, nr = plan.blocks(key)
        z0 = c0 = y0 = r0 = 0
        v = 1 if plan.split and key[0] is not None else 0
        y_low = None
        if plan.split:
            if key != (None, None):
                y_low = me == 0
        else:
            if key[0] is not None:
                z_low = my_z % 2 == 1 - key[0]
                z0 = jnp.where(z_low, 0, plan.z - nz)
                c0 = jnp.where(z_low, 0, plan.cz - nc)
            if key[1] is not None:
                y_low = my_y % 2 == 1 - key[1]
        if y_low is not None:
            y0 = jnp.where(y_low, 0, plan.y - ny)
            r0 = jnp.where(y_low, 0, plan.cy - nr)
        at = 0
        for i in range(nz):
            for j in range(ny):
                out_ref[at : at + plan.fold] = cells[v, z0 + i, y0 + j]
                at += plan.fold
        for i in range(nc):
            for j in range(nr):
                out_ref[at : at + half] = cots[v, c0 + i, r0 + j]
                at += half


def weight_kernel(plan, one_hbm, two_hbm, w1_ref, w2_ref, wb_ref, one_ref, two_ref, sems):
    loads = [
        pltpu.make_async_copy(one_hbm, one_ref, sems.at[0]),
        pltpu.make_async_copy(two_hbm, two_ref, sems.at[1]),
    ]
    for load in loads:
        load.start()
    for load in loads:
        load.wait()
    c_in, c_one, c_two = plan.c_in, plan.c_one, plan.c_two
    none = jnp.zeros((c_in, c_one), F32)
    pairs_x = {}
    for dz in range(3):
        for dy in range(3):
            tap = [one_ref[(dz * 3 + dy) * 3 + dx].astype(F32) * 0.5 for dx in range(3)]
            pairs_x[dz, dy, 0] = jnp.concatenate(
                [jnp.concatenate([tap[1], tap[0]], 1), jnp.concatenate([tap[2], tap[1]], 1)], 0
            )
            pairs_x[dz, dy, 1] = jnp.concatenate(
                [jnp.concatenate([none, tap[2]], 1), jnp.concatenate([tap[0], none], 1)], 0
            )
    blank = jnp.zeros((2 * c_in, 2 * c_one), F32)
    rows = []
    for fz in range(4):
        for s in range(2):
            for fy in (1, 2, 3, 0):
                rows.append(
                    jnp.concatenate(
                        [
                            pairs_x.get((fz - a, fy - b, s), blank)
                            for a in range(2)
                            for b in range(2)
                        ],
                        axis=1,
                    )
                )
    w1_ref[...] = jnp.concatenate(rows, axis=0).T.astype(BF16)
    for dx in range(3):
        taps = [two_ref[zy * 3 + dx] for zy in range(9)]
        wb_ref[dx * c_one : (dx + 1) * c_one] = jnp.concatenate(taps, axis=1)
        tall = jnp.concatenate([t.astype(F32) * 0.5 for t in taps], axis=0)
        w2_ref[dx * c_two : (dx + 1) * c_two] = tall.T.astype(BF16)


def around(ref, w, lane, size, step, sign):
    return jnp.concatenate(
        [
            ref[w + 1 + sign * dz, :, lane + sign * dy * step : lane + sign * dy * step + size]
            for dz in (-1, 0, 1)
            for dy in (-1, 0, 1)
        ],
        axis=0,
    )


def each(plan, count, body):
    if plan.split:
        for i in range(count):
            body(i, 0)
    else:
        lax.fori_loop(0, count, body, 0)


def forward_kernel(plan, count, *refs):
    msgs = refs[:count]
    w1_ref, w2_ref, keep_ref, give_ref, fine, act, sg, tan = refs[count : count + 8]
    cells, cot, sgx, total = refs[count + 8 :]
    X, Y, Z, R = plan.x, plan.y, plan.z, plan.r
    fold, c_in, c_one, c_two = plan.fold, plan.c_in, plan.c_one, plan.c_two
    me, my_z, my_y = lax.axis_index("pipe"), lax.axis_index("gz"), lax.axis_index("gy")
    own, first_sg = plan.at_z()
    row0 = plan.row0()
    low_ok, high_ok = my_y > 0, my_y < plan.gy - 1
    if plan.split:
        low_ok, high_ok = low_ok | (me == 1), high_ok | (me == 0)

    pick = (
        lax.broadcasted_iota(jnp.int32, (X, 2 * X), 1) // 2
        == lax.broadcasted_iota(jnp.int32, (X, 2 * X), 0)
    )
    pick = jnp.where(pick, 0.125, 0.0).astype(BF16)
    if not plan.split:
        cot[...] = jnp.zeros_like(cot)
    for kind, msg in zip(plan.kinds, msgs):
        nz, ny, nc, nr = plan.blocks(kind)
        z_kind, y_kind = kind
        below, used = None, None
        if plan.split:
            half = my_z if z_kind is None else 1 - my_z
            z0, c0 = half * Z, half * plan.cz + 1
            if y_kind is not None:
                below = me == 0
                used = (below & (my_y > 0)) | ((me == 1) & (my_y < plan.gy - 1))
        else:
            z0, c0 = own, 1
            if z_kind is not None:
                before = my_z % 2 == 1 - z_kind
                z0 = jnp.clip(jnp.where(before, own - plan.h, own + Z), 0, plan.win - plan.h)
                c0 = jnp.where(before, 0, plan.cz + 1)
            if y_kind is not None:
                below = my_y % 2 == 1 - y_kind
        y0, r0 = REACH, 0
        if y_kind is not None:
            y0 = jnp.where(below, 0, Y + REACH)
        elif z_kind is not None and plan.split:
            y0, r0 = REACH + me * (Y - ny), me * (plan.cy - nr)
        at = 0
        for i in range(nz):
            for j in range(ny):
                block = msg[at : at + fold]
                if used is not None:
                    block = jnp.where(used, block, jnp.zeros_like(block))
                cells[z0 + i, y0 + j] = block
                at += fold
        part = c_two // 2
        up = jnp.dot(msg[at : at + nc * nr * part], pick, preferred_element_type=F32)
        if used is not None:
            up = jnp.where(used, up, 0.0)
        up = up.astype(BF16)
        for i in range(nc):
            for j in range(nr):
                row = up[(i * nr + j) * part : (i * nr + j + 1) * part]
                if y_kind is None:
                    lanes = [(2 * (r0 + j) + 2) * X, (2 * (r0 + j) + 3) * X]
                else:
                    lanes = [jnp.where(below, X, (Y + 2) * X)]
                for lane in lanes:
                    lane = aligned(lane, X)
                    cot[c0 + i, :part, pl.ds(lane, X)] = row[:, :X]
                    cot[c0 + i, part:, pl.ds(lane, X)] = row[:, X:]

    quarter = 2 * c_in
    fine[0 : 8 * quarter] = jnp.zeros((8 * quarter, plan.mid * X), BF16)
    last = 8 * quarter + plan.win * 16 * quarter
    fine[last : last + 8 * quarter] = jnp.zeros((8 * quarter, plan.mid * X), BF16)
    is_c = (lax.broadcasted_iota(jnp.int32, (fold, X), 0) // c_in) % 2 == 1

    def spread(w, carry):
        base = aligned(8 * quarter + w * 16 * quarter, 8 * quarter)
        kept = []
        for r in range(plan.wide):
            mid = cells[w, row0 + r].astype(F32)
            side = jnp.where(is_c, shift(mid, 1, X), shift(mid, -1, X))
            kept.append((mid, side))
            if r < 2:
                continue
            lane = (r - 2) * X
            for a in range(2):
                for s in range(2):
                    lo, here, hi = kept[r - 2][s], kept[r - 1][s], kept[r][s]
                    at = a * 2 * quarter
                    near = here[at : at + 2 * quarter]
                    far = jnp.concatenate(
                        [hi[at : at + quarter], lo[at + quarter : at + 2 * quarter]], axis=0
                    )
                    row = base + (a * 8 + s * 4) * quarter
                    fine[pl.ds(row, 2 * quarter), lane : lane + X] = near.astype(BF16)
                    fine[pl.ds(row + 2 * quarter, 2 * quarter), lane : lane + X] = far.astype(BF16)
        return carry

    each(plan, plan.win, spread)

    w1 = w1_ref[...]
    last_q = plan.mid // 2 - 1
    act[0] = jnp.zeros(act.shape[1:], BF16)
    act[plan.win + 1] = jnp.zeros(act.shape[1:], BF16)

    def first_section(w, carry):
        top = aligned(w * 16 * quarter, 8 * quarter)
        z_abs = my_z * Z + w - own
        z_ok = None if plan.split else (z_abs >= 0) & (z_abs < plan.gz * Z)
        for q in range(plan.mid // 2):
            lane = 2 * q * X
            half = jnp.dot(
                w1, fine[pl.ds(top, 32 * quarter), lane : lane + 2 * X], preferred_element_type=F32
            )
            line, prod = None, None
            for g in range(8):
                v = half[g * c_one : (g + 1) * c_one]
                t = jnp.tanh(v)
                if 0 < q < last_q:
                    tan[w, g * c_one : (g + 1) * c_one, lane - 2 * X : lane] = t
                bent = jnp.maximum(v, LEAK * v)
                grown = 1.0 + jnp.abs(t)
                line = bent if line is None else line + bent
                prod = grown if prod is None else prod * grown
            mean = 0.25 * line - ((1.0 - LEAK) / 8.0) * jnp.log(prod)
            for ok in (z_ok, low_ok if q == 0 else None, high_ok if q == last_q else None):
                if ok is not None:
                    mean = jnp.where(ok, mean, 0.0)
            act[w + 1, :, lane : lane + 2 * X] = mean.astype(BF16)
        return carry

    each(plan, plan.win, first_section)

    w2 = w2_ref[...]
    sg[0] = jnp.zeros(sg.shape[1:], BF16)
    sg[plan.planes + 1] = jnp.zeros(sg.shape[1:], BF16)

    def second_section(j, carry):
        w = first_sg + j
        c_at = (w - own + 2) // 2
        taps = jnp.dot(w2, around(act, w, X, plan.slim * X, X, 1), preferred_element_type=F32)
        half = (
            taps[c_two : 2 * c_two]
            + shift(taps[:c_two], 1, X)
            + shift(taps[2 * c_two :], -1, X)
        )
        slope = (LEAK + 1.0) / 2 + ((1.0 - LEAK) / 2) * jnp.tanh(half)
        near = pl.multiple_of((row0 + 1) * X, X)
        part = cot[c_at, :, pl.ds(near, plan.slim * X)].astype(F32)
        sg[j + 1] = (slope * part).astype(BF16)
        return carry

    each(plan, plan.planes, second_section)

    grad_two = None
    for i in range(plan.o):
        w, j = own + i, own + i - first_sg
        for y in range(R):
            mid = sg[j + 1, :, (y + 1) * X : (y + 2) * X]
            wide = mid.astype(F32)
            at = slice(y * X, (y + 1) * X)
            sgx[0:c_two, at] = shift(wide, -1, X).astype(BF16)
            sgx[c_two : 2 * c_two, at] = mid
            sgx[2 * c_two : 3 * c_two, at] = shift(wide, 1, X).astype(BF16)
        term = lax.dot_general(
            around(act, w, 2 * X, R * X, X, 1),
            sgx[...],
            (((1,), (1,)), ((), ())),
            preferred_element_type=F32,
        )
        grad_two = term if grad_two is None else grad_two + term
    nine = 9 * c_one
    total[0:nine] = grad_two[:, : 2 * c_two]
    total[nine : nine + nine // 2] = jnp.concatenate(
        [grad_two[: nine // 2, 2 * c_two :], grad_two[nine // 2 :, 2 * c_two :]], axis=1
    )
    rest = total.shape[0] - nine - nine // 2
    if rest > 0:
        total[nine + nine // 2 :] = jnp.zeros((rest, total.shape[1]), F32)
    rows = total.shape[0] // 2
    keep_ref[...] = total[pl.ds(pl.multiple_of(me * rows, rows), rows)]
    give_ref[...] = total[pl.ds(pl.multiple_of((1 - me) * rows, rows), rows)].astype(BF16)


def backward_kernel(plan, wb_ref, fine, act, sg, tan, one_ref, *refs):
    out_refs, (back, first) = refs[:-2], refs[-2:]
    X, Z, R = plan.x, plan.z, plan.r
    c_in, c_one = plan.c_in, plan.c_one
    quarter = 2 * c_in
    own, first_sg = plan.at_z()
    wb = wb_ref[...]
    tall = []
    for i in range(plan.o):
        w, j = own + i, own + i - first_sg
        for q in range(R // 2):
            lane = 2 * q * X
            taps = jnp.dot(wb, around(sg, j, lane + X, 2 * X, X, -1), preferred_element_type=F32)
            grad = (
                taps[c_one : 2 * c_one]
                + shift(taps[:c_one], -1, X)
                + shift(taps[2 * c_one :], 1, X)
            ).astype(BF16)
            back[i, :, lane : lane + 2 * X] = grad
            grad = grad.astype(F32) * 0.125
            for g in range(8):
                t = tan[w, g * c_one : (g + 1) * c_one, lane : lane + 2 * X]
                slope = (LEAK + 1.0) / 2 + ((1.0 - LEAK) / 2) * t
                at = (i * R + 2 * q) * X
                first[g * c_one : (g + 1) * c_one, at : at + 2 * X] = (slope * grad).astype(BF16)
        top = aligned(w * 16 * quarter, 8 * quarter)
        tall.append(fine[pl.ds(top, 32 * quarter), 2 * X : (2 + R) * X])
    grad_one = lax.dot_general(
        jnp.concatenate(tall, axis=1),
        first[...],
        (((1,), (1,)), ((), ())),
        preferred_element_type=F32,
    )
    half = 4 * c_one
    third = 8 * quarter
    folded = grad_one[: 3 * third, :half] + grad_one[third:, half:]
    place = {1: 0, 2: 1, 3: 2, 0: 3}

    def piece(dz, s, fy):
        row = dz * third + (s * 4 + place[fy]) * quarter
        return folded[row : row + quarter]

    taps = []
    up, down = slice(0, c_in), slice(c_in, 2 * c_in)
    left, right = slice(0, c_one), slice(c_one, 2 * c_one)
    for dz in range(3):
        for dy in range(3):
            mid, side = (
                piece(dz, s, dy)[:, : half // 2] + piece(dz, s, dy + 1)[:, half // 2 :]
                for s in range(2)
            )
            taps.append(side[down, left] + mid[up, right])
            taps.append(mid[up, left] + mid[down, right])
            taps.append(mid[down, left] + side[up, right])
    per = one_ref.shape[1] // c_one
    taps += [jnp.zeros((c_in, c_one), F32)] * (-len(taps) % (2 * per))
    for at in range(0, len(taps), 2 * per):
        pair = [jnp.concatenate(taps[at + k : at + k + per], axis=1) for k in (0, per)]
        row = at // per * c_in
        one_ref[row : row + 2 * c_in] = jnp.concatenate(pair, axis=0)
    done = len(taps) // per * c_in
    if done < one_ref.shape[0]:
        one_ref[done:] = jnp.zeros((one_ref.shape[0] - done, one_ref.shape[1]), F32)

    for k, out_ref in enumerate(out_refs):
        z0 = 0
        if plan.split:
            my_z = lax.axis_index("gz")
            z0 = (my_z if k == 0 else 1 - my_z) * Z
        for i in range(Z):
            for y in range(R):
                out_ref[0, i, y] = act[own + z0 + i + 1, :, (2 + y) * X : (3 + y) * X]
                out_ref[1, i, y] = back[z0 + i, :, y * X : (y + 1) * X]


def join_kernel(plan, *refs):
    parts, outs = refs[:-2], refs[-2:]
    me = lax.axis_index("pipe")
    my_z = lax.axis_index("gz")
    for i in range(plan.z):
        for kind, out_ref in enumerate(outs):
            if plan.split:
                mine, theirs, mine_far, theirs_far = parts
                for v, (here, far) in enumerate(((mine, mine_far), (theirs, theirs_far))):
                    one, two = here[kind, i].astype(F32), far[kind, i].astype(F32)
                    low, high = jnp.where(me == 0, one, two), jnp.where(me == 0, two, one)
                    lines = jnp.concatenate([low, high], axis=0)
                    at = my_z if v == 0 else 1 - my_z
                    out_ref[at, :, i] = jnp.swapaxes(lines, 0, 1).astype(BF16)
            else:
                for v, part in enumerate(parts):
                    at = me if v == 0 else 1 - me
                    lines = part[kind, i].astype(F32)
                    out_ref[at, :, i] = jnp.swapaxes(lines, 0, 1).astype(BF16)


def unpack_kernel(plan, own_ref, other_ref, one_hbm, two_hbm, one_ref, two_ref, full, sems):
    c_in, c_one, c_two = plan.c_in, plan.c_one, plan.c_two
    me = lax.axis_index("pipe")
    rows = full.shape[0] // 2
    scale = 1.0 / plan.batch
    full[pl.ds(pl.multiple_of(me * rows, rows), rows)] = own_ref[:rows] * scale
    full[pl.ds(pl.multiple_of((1 - me) * rows, rows), rows)] = other_ref[:rows] * scale
    nine = 9 * c_one
    part = c_one // 2
    stores = []
    for zy in range(9):
        block = full[zy * c_one : (zy + 1) * c_one]
        two_ref[zy * 3] = block[:, :c_two]
        two_ref[zy * 3 + 1] = block[:, c_two:]
        for p in (2 * zy, 2 * zy + 1):
            at = nine + (p % 9) * part
            lane = (p // 9) * c_two
            two_ref[zy * 3 + 2, (p % 2) * part : (p % 2 + 1) * part] = full[
                at : at + part, lane : lane + c_two
            ]
        if zy % STEP == STEP - 1:
            at = pl.ds((zy - STEP + 1) * 3, 3 * STEP)
            stores.append(pltpu.make_async_copy(two_ref.at[at], two_hbm.at[at], sems.at[len(stores)]))
            stores[-1].start()
    ones = (own_ref[rows:] + other_ref[rows:]) * scale
    per = ones.shape[1] // c_one
    for t in range(27):
        row, lane = t // per * c_in, t % per * c_one
        one_ref[t] = ones[row : row + c_in, lane : lane + c_one]
    stores.append(pltpu.make_async_copy(one_ref, one_hbm, sems.at[len(stores)]))
    stores[-1].start()
    for store in stores:
        store.wait()


def vmem(count):
    return [pl.BlockSpec(memory_space=pltpu.VMEM)] * count


def shape(dims, dtype):
    return jax.ShapeDtypeStruct(dims, dtype)


def bits(axis):
    return [(axis, 1 << k) for k in range((lax.axis_size(axis) - 1).bit_length())]


def partner(plan, part, moves, other_moves=None):
    perm = []
    for d in range(plan.dp):
        for p in range(plan.pipe):
            for a in range(plan.gz):
                for c in range(plan.gy):
                    to = {"dp": d, "pipe": p, "gz": a, "gy": c}
                    for axis, step in moves if p == 0 or other_moves is None else other_moves:
                        to[axis] ^= step
                    perm.append((plan.index(d, p, a, c), plan.index(*to.values())))
    return lax.ppermute(part, AXES, perm)


def sum_replicas(plan, part):
    moves = bits("dp") + bits("gz") + bits("gy")
    steps = [moves[i : i + 2] for i in range(0, len(moves), 2)]
    if any(len(step) == 1 for step in steps):
        orders = zip(steps, steps)
    else:
        orders = zip(steps[::-1], steps)
    for here, there in orders:
        sent = part.astype(BF16)
        got = [partner(plan, sent, here[:1], there[:1]).astype(F32)]
        if len(here) > 1:
            got.append(partner(plan, sent, here[1:], there[1:]).astype(F32))
            got.append(partner(plan, sent, here, there).astype(F32))
        part = sent.astype(F32) + got[0]
        if len(here) > 1:
            part = part + (got[1] + got[2])
    return part


def per_device(volumes, conv_one, conv_two, cotangent):
    plan = Plan(volumes, cotangent, conv_one, conv_two)
    X, Y, Z, R = plan.x, plan.y, plan.z, plan.r
    c_in, c_one, c_two = plan.c_in, plan.c_one, plan.c_two
    keys = sorted({message_key(plan, k) for k in plan.kinds}, key=str)
    count = 2 if plan.split else 1
    sent = pl.pallas_call(
        functools.partial(pack_kernel, plan, keys),
        out_shape=[shape((plan.rows(k), X), BF16) for k in keys],
        in_specs=[pl.BlockSpec(memory_space=pltpu.HBM)] * 2,
        out_specs=vmem(len(keys)),
        scratch_shapes=[
            pltpu.VMEM((count,) + volumes.shape[1:], BF16),
            pltpu.VMEM((count,) + cotangent.shape[1:], BF16),
            pltpu.VMEM((count, Z, Y, plan.fold, X), BF16),
            pltpu.VMEM((count, plan.cz, plan.cy, c_two // 2, X), BF16),
            pltpu.SemaphoreType.DMA((2 * count,)),
        ],
        compiler_params=PARAMS,
        name="pack",
    )(*[pltpu.with_memory_space_constraint(a, pltpu.HBM) for a in (volumes, cotangent)])
    sent = dict(zip(keys, sent))
    msgs = []
    for kind in plan.kinds:
        cells = sent[message_key(plan, kind)]
        msgs.append(cells if kind == (None, None) else swap(cells, plan, kind))

    w1, w2, wb = pl.pallas_call(
        functools.partial(weight_kernel, plan),
        out_shape=[
            shape((8 * c_one, 64 * c_in), BF16),
            shape((3 * c_two, 9 * c_one), BF16),
            shape((3 * c_one, 9 * c_two), BF16),
        ],
        in_specs=[pl.BlockSpec(memory_space=pltpu.HBM)] * 2,
        out_specs=vmem(3),
        scratch_shapes=[
            pltpu.VMEM((27, c_in, c_one), BF16),
            pltpu.VMEM((27, c_one, c_two), BF16),
            pltpu.SemaphoreType.DMA((2,)),
        ],
        compiler_params=PARAMS,
        cost_estimate=pl.CostEstimate(flops=10**7, bytes_accessed=10**6, transcendentals=0),
        name="weights",
    )(
        *[
            pltpu.with_memory_space_constraint(
                w.transpose(2, 3, 4, 1, 0).reshape(27, w.shape[1], w.shape[0]), pltpu.HBM
            )
            for w in (conv_one, conv_two)
        ]
    )

    wide = 2 * c_two
    two_rows = -(-27 * c_one // 64) * 16
    one_rows = -(-27 * c_in * c_one // (16 * wide)) * 16
    keep, give, fine, act, sg, tan = pl.pallas_call(
        functools.partial(forward_kernel, plan, len(msgs)),
        out_shape=[
            shape((two_rows, wide), F32),
            shape((two_rows, wide), BF16),
            shape(((plan.win + 1) * 32 * c_in, plan.mid * X), BF16),
            shape((plan.win + 2, c_one, plan.mid * X), BF16),
            shape((plan.planes + 2, c_two, plan.slim * X), BF16),
            shape((plan.win, 8 * c_one, R * X), F32),
        ],
        in_specs=vmem(len(msgs) + 2),
        out_specs=vmem(6),
        scratch_shapes=[
            pltpu.VMEM((plan.win, Y + 2 * REACH, plan.fold, X), BF16),
            pltpu.VMEM((plan.cot_planes, c_two, (Y + 4) * X), BF16),
            pltpu.VMEM((3 * c_two, R * X), BF16),
            pltpu.VMEM((2 * two_rows, wide), F32),
        ],
        compiler_params=PARAMS,
        name="forward",
    )(*msgs, w1, w2)

    both = [("pipe", 1)]
    part = keep + partner(plan, give, both).astype(F32)
    blocks = shape((2, Z, R, c_one, X), BF16)
    one, *outs = pl.pallas_call(
        functools.partial(backward_kernel, plan),
        out_shape=[shape((one_rows, wide), F32)] + [blocks] * (2 if plan.split else 1),
        in_specs=vmem(5),
        out_specs=vmem(3 if plan.split else 2),
        scratch_shapes=[
            pltpu.VMEM((plan.o, c_one, R * X), BF16),
            pltpu.VMEM((8 * c_one, plan.o * R * X), BF16),
        ],
        compiler_params=PARAMS,
        cost_estimate=pl.CostEstimate(flops=10**9, bytes_accessed=10**7, transcendentals=0),
        name="backward",
    )(wb, fine, act, sg, tan)

    part = sum_replicas(plan, jnp.concatenate([part, one], axis=0))
    rest = partner(plan, part, both)
    if plan.split:
        outs = [outs[0], partner(plan, outs[1], [("gz", 1)])]
    outs = outs + [partner(plan, out, both) for out in outs]
    size = (2, c_one, Z, Y, X)
    all_act, all_back = pl.pallas_call(
        functools.partial(join_kernel, plan),
        out_shape=[shape(size, BF16)] * 2,
        in_specs=vmem(len(outs)),
        out_specs=vmem(2),
        compiler_params=PARAMS,
        name="join",
    )(*outs)
    grad_one, grad_two = pl.pallas_call(
        functools.partial(unpack_kernel, plan),
        out_shape=[shape((27, c_in, c_one), F32), shape((27, c_one, c_two), F32)],
        in_specs=vmem(2),
        out_specs=[pl.BlockSpec(memory_space=pltpu.HBM)] * 2,
        scratch_shapes=[
            pltpu.VMEM((27, c_in, c_one), F32),
            pltpu.VMEM((27, c_one, c_two), F32),
            pltpu.VMEM((2 * two_rows, wide), F32),
            pltpu.SemaphoreType.DMA((9 // STEP + 1,)),
        ],
        compiler_params=PARAMS,
        name="unpack",
    )(part, rest)
    grad_one = grad_one.reshape(3, 3, 3, c_in, c_one).transpose(4, 3, 0, 1, 2)
    grad_two = grad_two.reshape(3, 3, 3, c_one, c_two).transpose(4, 3, 0, 1, 2)
    return all_act, all_back, grad_one, grad_two


def solution(mesh):
    in_specs = (P("dp", None, "gz", "gy", None), P(), P(), P("dp", None, "gz", "gy", None))
    out_specs = (P("dp", None, "gz", "gy", None), P("dp", None, "gz", "gy", None), P(), P())
    return jax.shard_map(
        per_device, mesh=mesh, in_specs=in_specs, out_specs=out_specs, check_vma=False
    )
```
